256 devices in a mesh: pts: 64 (over x, z, core), cam: 4 (over y).
Axes of the slice: x: 4, y: 4, z: 8, core: 2. Of those that a mesh axis runs over, the one named last changes fastest.
Arguments:
- jac_cam: float32 [4, 2, 6, 524288], P(None, None, None, ('pts', 'cam')), may hold values from -0.6 to 0.6
- jac_pt: float32 [4, 2, 3, 524288], P(None, None, None, ('pts', 'cam')), may hold values from -3 to 3
- resid: float32 [4, 2, 524288], P(None, None, ('pts', 'cam')), may hold values from -6 to 6
- point_damping: float32 [524288], P(('pts', 'cam')), may hold values from 0.5 to 4
- cluster: int32 [524288, 1], P(('pts', 'cam')), may hold values from 0 to 63; in each aligned block of 2048 rows (0 to 2047, 2048 to 4095, ...) at most 64 rows name the same one
- cam_local: int32 [524288, 4], P(('pts', 'cam')), may hold values from 0 to 511, all different within a row
- direction: float32 [6, 32768], P(None, ('pts', 'cam')), may hold values from -6 to 6
- cam_damping: float32 [32768], P(('pts', 'cam')), may hold values from 0.5 to 4
Outputs:
- grad_reduced: float32 [6, 32768], P(None, ('pts', 'cam'))
- schur_dir: float32 [6, 32768], P(None, ('pts', 'cam'))
The draws below stay inside these ranges and needn't reach their ends.
Inputs may be any that keep to these rules, and one draw needn't show every extreme that they name: In the block of 2048 points of one device no cluster is seen by more than 64 points, a bound that some block reaches. `cam_local`: the 4 cameras of one point are distinct.
All inputs are finite; a program needn't handle non-finite values.
Results may differ from the reference program's by a relative error of at most 0.00011.
Values sent between devices are 32-bit elements; how exact they have to be, the bound alone decides.
A program may use at most 64 MiB of HBM per device.

```python
import math
import jax
import jax.numpy as jnp
import numpy as np
from jax import lax

K = 4
CL = 512
P_DEV = 2048
CAP = 64
POINTS = 524288
CAMS = 32768
N_PTS = 64


def level_of(key, dims, pieces, smallest, largest):
    def one(dim, blocks):
        heights = jax.random.uniform(jax.random.fold_in(jax.random.fold_in(key, 6), dim), (blocks,), jnp.float32, smallest / len(pieces), largest / len(pieces))
        return jnp.repeat(jnp.exp(heights), dims[dim] // blocks).reshape((-1,) + (1,) * (len(dims) - dim - 1))

    factor_of = one(*pieces[0])
    for cut in pieces[1:]:
        factor_of = factor_of * one(*cut)
    return factor_of


def different_ones(own_key, rows, number_of, top, lift):
    ranking = jax.random.permutation(jax.random.fold_in(own_key, 1), number_of)
    pull = ranking
    for power in range(3):
        pull = pull * pull // number_of
    pull = pull * lift // number_of
    tickets = jax.random.randint(jax.random.fold_in(own_key, 2), (rows, number_of), 0, 4096) + pull
    holders = jax.random.permutation(jax.random.fold_in(own_key, 3), rows)[jnp.arange(number_of) % rows]
    tickets = jnp.where(jnp.arange(rows)[:, None] == holders[None, :], 1 << 14, tickets)
    score = tickets * number_of + jnp.arange(number_of)
    return lax.top_k(score.astype(jnp.int32), top)[1].astype(jnp.int32)


def shared_out(key, own, number, rows, count, top, bound, lean):
    ranking = jax.random.permutation(key, count)
    heavy_load, usual = shares(count, rows * top, bound, lean, True), shares(count, rows * top, bound, lean, False)
    places = jnp.arange(count)

    def named(sizes, rotation):
        used = int((sizes > 0).sum())
        fixed = max(1, used // 4)
        moved = fixed + (places - fixed + rotation * (used - fixed)) % max(1, count - fixed)
        return jnp.zeros((count,), jnp.int32).at[ranking[jnp.where(places < fixed, places, moved)]].set(jnp.asarray(sizes, jnp.int32))

    sizes = jnp.where(number % 4 == 0, named(heavy_load, number // 4), named(usual, number - number // 4 - 1))
    mixed = jax.random.permutation(jax.random.fold_in(own, 3), count)
    source_of, sink = mixed[0:count // 2 * 2:2], mixed[1:count // 2 * 2:2]
    slack = jnp.minimum(sizes[source_of] - 1, bound - sizes[sink]) // 2
    slack = jnp.where((source_of == ranking[0]) | (sink == ranking[0]) | (sizes[sink] == 0), 0, jnp.maximum(slack, 0))
    moved = jax.random.randint(jax.random.fold_in(own, 4), (count // 2,), 0, 1 << 20) % (slack + 1)
    sizes = sizes.at[source_of].add(-moved).at[sink].add(moved)
    labels = jnp.searchsorted(jnp.cumsum(sizes), jnp.arange(rows * top), side="right").astype(jnp.int32)
    table = labels.reshape(top, rows).T
    table = table[jax.random.permutation(jax.random.fold_in(own, 1), rows)]
    rotation = jax.random.randint(jax.random.fold_in(own, 2), (rows, 1), 0, top)
    return jnp.take_along_axis(table, (jnp.arange(top)[None, :] + rotation) % top, axis=1)


def shares(number_of, total, bound, skew, full):
    portions = [(1 << 20) // math.isqrt(standing ** skew) + 1 for standing in range(1, number_of + 1)]
    largest = bound if full else min(bound, max(-(-total // number_of), total * portions[0] // sum(portions)))
    least = 1 if total - largest >= number_of - 1 else 0
    holding, spare = [largest] + [least] * (number_of - 1), total - largest - least * (number_of - 1)
    while spare > 0:
        free = [i for i in range(1, number_of) if holding[i] < largest] or [i for i in range(1, number_of) if holding[i] < bound]
        mass, budget = sum([portions[i] for i in free]), spare
        for i in free:
            extra = min(bound - holding[i], max(1, budget * portions[i] // mass), spare)
            holding[i] = holding[i] + extra
            spare = spare - extra
    return np.array(holding)


def scatter_about(key, extent, deviation, most, shards=(), held_as=jnp.bfloat16):
    entries = deviation * jax.random.normal(key, extent, jnp.float32)
    if shards:
        entries = entries * level_of(key, extent, shards, -0.22, 0.18)
    return jnp.clip(entries, -most, most).astype(held_as)


def setup_inputs(seed: int = 0) -> dict:
    splits = jax.random.split(jax.random.key(seed), 9)
    jac_cam = scatter_about(splits[0], (K, 2, 6, POINTS), 0.1, 0.6, ((3, 256),), jnp.float32)
    jac_pt = scatter_about(splits[1], (K, 2, 3, POINTS), 0.5, 3.0, ((3, 256),), jnp.float32)
    resid = scatter_about(splits[2], (K, 2, POINTS), 1.0, 6.0, ((2, 256),), jnp.float32)
    point_damping = jnp.clip(jnp.exp(math.log(4.0) - 2.0794415 * jax.random.uniform(splits[3], (POINTS,), jnp.float32) ** level_of(splits[3], (POINTS,), ((0, 256),), -0.2, 0.2)), 0.5, 4.0)
    cluster_keys = jax.random.split(jax.random.fold_in(splits[4], 1), POINTS // P_DEV)
    cluster_turns = jax.random.permutation(jax.random.fold_in(splits[4], 3), POINTS // P_DEV)
    cluster = jax.vmap(lambda own, number: shared_out(jax.random.fold_in(splits[4], 2), own, number, P_DEV, N_PTS, 1, CAP, 2))(cluster_keys, cluster_turns).reshape((POINTS, 1))
    cam_local = different_ones(splits[5], POINTS, CL, K, 64)
    direction = scatter_about(splits[6], (6, CAMS), 1.0, 6.0, ((1, 256),), jnp.float32)
    cam_damping = jnp.clip(jnp.exp(math.log(4.0) - 2.0794415 * jax.random.uniform(splits[7], (CAMS,), jnp.float32) ** level_of(splits[7], (CAMS,), ((0, 256),), -0.2, 0.2)), 0.5, 4.0)
    return dict(jac_cam=jac_cam, jac_pt=jac_pt, resid=resid, point_damping=point_damping, cluster=cluster, cam_local=cam_local, direction=direction, cam_damping=cam_damping)


def factor_parts(normal):
    diag_a = jnp.sqrt(normal[0, 0])
    off_ba = normal[1, 0] / diag_a
    off_ca = normal[2, 0] / diag_a
    diag_b = jnp.sqrt(normal[1, 1] - off_ba * off_ba)
    off_cb = (normal[2, 1] - off_ca * off_ba) / diag_b
    diag_c = jnp.sqrt(normal[2, 2] - off_ca * off_ca - off_cb * off_cb)
    return (diag_a, off_ba, off_ca, diag_b, off_cb, diag_c)

def lower_solve(parts, values):
    diag_a, off_ba, off_ca, diag_b, off_cb, diag_c = parts
    first = values[..., 0, :] / diag_a
    second = (values[..., 1, :] - off_ba * first) / diag_b
    third = (values[..., 2, :] - off_ca * first - off_cb * second) / diag_c
    return jnp.stack([first, second, third], axis=-2)

def eliminate(jac_cam, jac_pt, resid, damping):
    identity = jnp.eye(3, dtype=jnp.float32)[:, :, None]
    normal = lax.optimization_barrier(jnp.sum(jac_pt[:, :, :, None, :] * jac_pt[:, :, None, :, :], axis=(0, 1))) + damping[None, None, :] * identity
    rhs_sum = lax.optimization_barrier(jnp.sum(jac_pt * resid[:, :, None, :], axis=(0, 1)))
    cross = lax.optimization_barrier(jnp.sum(jac_cam[:, :, :, None, :] * jac_pt[:, :, None, :, :], axis=1))
    parts = factor_parts(normal)
    reduced = lower_solve(parts, cross)
    solved = lower_solve(parts, rhs_sum)
    grad_obs = lax.optimization_barrier(jnp.sum(jac_cam * resid[:, :, None, :], axis=1)) - lax.optimization_barrier(jnp.sum(reduced * solved[None, None, :, :], axis=2))
    return (reduced, grad_obs)

def apply_terms(jac_cam, reduced, dir_obs):
    projected = lax.optimization_barrier(jnp.sum(reduced * dir_obs[:, :, None, :], axis=(0, 1)))
    image = lax.optimization_barrier(jnp.sum(jac_cam * dir_obs[:, None, :, :], axis=2))
    returned = lax.optimization_barrier(jnp.sum(jac_cam * image[:, :, None, :], axis=1))
    return returned - lax.optimization_barrier(jnp.sum(reduced * projected[None, None, :, :], axis=2))

def reference(jac_cam, jac_pt, resid, point_damping, cluster, cam_local, direction, cam_damping):
    reduced, grad_obs = eliminate(jac_cam, jac_pt, resid, point_damping)
    camera_ids = (cluster[:, 0][None, :] * CL + cam_local.T).astype(jnp.int32)
    dir_obs = jnp.transpose(direction[:, camera_ids], (1, 0, 2))
    contrib = apply_terms(jac_cam, reduced, dir_obs)
    flat_ids = camera_ids.reshape(-1)

    def spread(values):
        table = jnp.transpose(values, (0, 2, 1)).reshape(-1, 6)
        return jax.ops.segment_sum(table, flat_ids, num_segments=CAMS).T
    grad_reduced = spread(grad_obs)
    schur_dir = cam_damping[None, :] * direction + spread(contrib)
    return (grad_reduced, schur_dir)
```

```python
import jax
import jax.numpy as jnp
from jax import lax
from jax.experimental import pallas as pl
from jax.experimental.pallas import tpu as pltpu
from jax.sharding import PartitionSpec as P

MESH = pl.DeviceIdType.MESH
F32 = jnp.float32
BF16 = jnp.bfloat16
NX, NY, NZ, NC = 4, 4, 8, 2
POINTS = 2048
CHUNK = 256
ROWS = 176
TRACK = 4
TRANSPOSED = (((1,), (1,)), ((), ()))


def split(value):
    high = value.astype(BF16)
    low = (value - high.astype(F32)).astype(BF16)
    return high, low


def kernel(
    jc_ref, jp_ref, rs_ref, damp_ref, clu_ref, loc_ref, dir_ref, cdamp_ref,
    og_ref, os_ref,
    bt, rt, srow, lhs, sb, lb, db, vb, ohb, tt,
    zb, p0, qa, qb, ra, rb,
    gbuf, sbuf, in1g, in1s, r1ag, r1bg, r1as, r1bs, in2ag, in2bg, in2as, in2bs,
    r2ag, r2bg, r2as, r2bs, in3ag, in3bg, in3as, in3bs, r3g, r3s, r4g, r4s, in4g, in4s,
    send, recv,
):
    me = lax.axis_index("pts")
    y = lax.axis_index("cam")
    core = lax.rem(me, NC)
    z = lax.rem(lax.div(me, NC), NZ)
    x = lax.div(me, NC * NZ)

    def device(xx, yy, zz, cc):
        return {"pts": (xx * NZ + zz) * NC + cc, "cam": yy}

    def step(at, d, size):
        return lax.rem(at + d, size)

    def rows(ref, start, count):
        return ref.at[pl.ds(pl.multiple_of(start, 8), count), :]

    def copy(src, dst, sem, dev):
        return pltpu.make_async_remote_copy(
            src_ref=src, dst_ref=dst, send_sem=send.at[sem], recv_sem=recv.at[sem],
            device_id=dev, device_id_type=MESH,
        )

    def gather_z():
        return [
            copy(dir_ref, rows(zb, z * 8, 6), d - 1, device(x, y, step(z, d, NZ), core))
            for d in range(1, NZ)
        ]

    def gather_first():
        return [
            copy(rows(p0, 0, 24), rows(qa, x * 24, 24), 6 + d, device(step(x, d, NX), y, z, core))
            for d in range(1, NX)
        ] + [
            copy(rows(p0, 24, 24), rows(qb, y * 24, 24), 9 + d, device(x, step(y, d, NY), z, core))
            for d in range(1, NY)
        ]

    def gather_second():
        return [
            copy(qa, rows(ra, (core * NY + y) * 96, 96), 12 + d,
                 device(x, step(y, d, NY), z, core))
            for d in range(1, NY)
        ] + [
            copy(qb, rows(rb, (x * NC + core) * 96, 96), 15 + d,
                 device(step(x, d, NX), y, z, core))
            for d in range(1, NX)
        ]

    def gather_core():
        other = device(x, y, z, 1 - core)
        mine = rows(ra, core * 384, 384)
        out = [copy(mine, mine, 19, other)]
        for xx in range(NX):
            part = rows(rb, (xx * NC + core) * 96, 96)
            out.append(copy(part, part, 20 + xx, other))
        return out

    def sum_core(base, dense, in1, xx):
        return copy(
            rows(dense, (xx * NC + 1 - core) * 192, 192), rows(in1, xx * 192, 192),
            base + xx, device(x, y, z, 1 - core),
        )

    def sum_first(base, r1a, r1b, in2a, in2b):
        return [
            copy(rows(r1a, step(x, d, NX) * 96, 96), rows(in2a, x * 96, 96), base + 3 + d,
                 device(step(x, d, NX), y, z, core))
            for d in range(1, NX)
        ] + [
            copy(rows(r1b, step(y, d, NY) * 96, 96), rows(in2b, y * 96, 96), base + 6 + d,
                 device(x, step(y, d, NY), z, core))
            for d in range(1, NY)
        ]

    def sum_second(base, r2a, r2b, in3a, in3b):
        return [
            copy(rows(r2a, step(y, d, NY) * 24, 24), rows(in3a, y * 24, 24), base + 9 + d,
                 device(x, step(y, d, NY), z, core))
            for d in range(1, NY)
        ] + [
            copy(rows(r2b, step(x, d, NX) * 24, 24), rows(in3b, x * 24, 24), base + 12 + d,
                 device(step(x, d, NX), y, z, core))
            for d in range(1, NX)
        ]

    def sum_z(base, r4, in4):
        return [
            copy(rows(r4, step(z, d, NZ) * 8, 8), rows(in4, z * 8, 8), base + 15 + d,
                 device(x, y, step(z, d, NZ), core))
            for d in range(1, NZ)
        ]

    def start(copies):
        for item in copies:
            item.start()

    def wait(copies):
        for item in copies:
            item.wait()

    def fold_core(dense, in1, r1a, r1b):
        for xx in range(NX):
            total = (
                dense[pl.ds(pl.multiple_of((xx * NC + core) * 192, 8), 192), :]
                + in1[pl.ds(xx * 192, 192), :]
            )
            for yy in range(NY):
                r1a[pl.ds(xx * 96 + yy * 24, 24), :] = total[yy * 48:yy * 48 + 24]
                r1b[pl.ds(yy * 96 + xx * 24, 24), :] = total[yy * 48 + 24:yy * 48 + 48]

    def fold(own, arrived, at, size, count):
        total = own[pl.ds(pl.multiple_of(at * count, 8), count), :]
        for d in range(1, size):
            total += arrived[pl.ds(pl.multiple_of(step(at, d, size) * count, 8), count), :]
        return total

    barrier = pltpu.get_barrier_semaphore()
    peers = [device(step(x, d, NX), y, z, core) for d in range(1, NX)]
    peers += [device(x, step(y, d, NY), z, core) for d in range(1, NY)]
    peers += [device(x, y, step(z, d, NZ), core) for d in range(1, NZ)]
    peers += [device(x, y, z, 1 - core)]
    for dev in peers:
        pl.semaphore_signal(barrier, inc=1, device_id=dev, device_id_type=MESH)

    for kk in range(8):
        for b in range(POINTS // 128):
            bt[b, pl.ds(kk, 3, stride=8), :] = jp_ref[kk, :, pl.ds(b * 128, 128)]
    for kk in range(TRACK):
        rt[pl.ds(2 * kk, 2), :] = rs_ref[kk]
    tt[...] = jnp.zeros_like(tt)
    r4g[...] = jnp.zeros_like(r4g)
    r4s[...] = jnp.zeros_like(r4s)

    pl.semaphore_wait(barrier, len(peers))
    start(gather_z())

    lane = lax.broadcasted_iota(jnp.int32, (CHUNK, CHUNK + 128), 1)
    before = (
        (lax.broadcasted_iota(jnp.int32, (CHUNK, CHUNK + 128), 0) < lane) | (lane >= CHUNK)
    ).astype(F32).astype(BF16)

    def eliminate(b, seen):
        here = pl.ds(pl.multiple_of(b * CHUNK, CHUNK), CHUNK)
        cluster = clu_ref[:, here]
        member = (
            lax.broadcasted_iota(jnp.int32, (64, CHUNK), 0) == jnp.broadcast_to(cluster, (64, CHUNK))
        ).astype(F32)
        counts = jnp.dot(member.astype(BF16), before, preferred_element_type=F32)
        ahead = counts[:, :CHUNK] + jnp.concatenate([seen, seen], axis=1)
        position = jnp.sum(member * ahead, axis=0, keepdims=True)
        slot = jnp.bitwise_and(cluster, 15) * 64 + position.astype(jnp.int32)
        srow[:, here] = slot
        quarter = lax.shift_right_logical(cluster, 4)

        b0, b1, b2 = (
            jnp.concatenate([bt[2 * b + i, pl.ds(8 * j, 8), :] for i in range(2)], axis=1)
            for j in range(3)
        )
        res = rt[:, here]

        def total(value):
            return jnp.sum(value, axis=0, keepdims=True)

        damp = damp_ref[:, here]
        n00, n10, n20 = total(b0 * b0) + damp, total(b1 * b0), total(b2 * b0)
        n11, n21, n22 = total(b1 * b1) + damp, total(b2 * b1), total(b2 * b2) + damp
        q0, q1, q2 = total(b0 * res), total(b1 * res), total(b2 * res)
        ia = 1.0 / jnp.sqrt(n00)
        ba, ca = n10 * ia, n20 * ia
        ib = 1.0 / jnp.sqrt(n11 - ba * ba)
        cb = (n21 - ca * ba) * ib
        ic = 1.0 / jnp.sqrt(n22 - ca * ca - cb * cb)
        c0 = b0 * ia
        c1 = (b1 - ba * c0) * ib
        c2 = (b2 - ca * c0 - cb * c1) * ic
        s0 = q0 * ia
        s1 = (q1 - ba * s0) * ib
        s2 = (q2 - ca * s0 - cb * s1) * ic
        rest = res - (c0 * s0 + c1 * s1 + c2 * s2)

        masks = [
            jnp.broadcast_to((quarter == f).astype(F32), (16, CHUNK)).astype(BF16)
            for f in range(NX)
        ]

        def put(base, value):
            for f in range(NX):
                lhs[pl.ds(f * ROWS + base, 16), here] = value * masks[f]

        for pair in range(4):
            parts = []
            for kk in (2 * pair, 2 * pair + 1):
                parts += [jc_ref[kk, :, here], c0[kk:kk + 1], c1[kk:kk + 1]]
            high, low = split(jnp.concatenate(parts, axis=0))
            put(16 * pair, high)
            put(80 + 16 * pair, low)
        high, low = split(jnp.concatenate([c2, rest], axis=0))
        put(64, high)
        put(144, low)
        label = loc_ref[:, here]
        parts = [
            lax.shift_right_logical(label, 7).astype(F32),
            jnp.bitwise_and(label, 127).astype(F32),
            jnp.zeros((8, CHUNK), F32),
        ]
        put(160, jnp.concatenate(parts, axis=0).astype(BF16))
        return seen + counts[:, CHUNK:]

    lax.fori_loop(0, POINTS // CHUNK, eliminate, jnp.zeros((64, 128), F32))

    wait(gather_z())
    zb[pl.ds(pl.multiple_of(z * 8, 8), 6), :] = dir_ref[...]
    for zz in range(NZ):
        p0[pl.ds(zz, 6, stride=8), :] = zb[pl.ds(zz * 8, 6), :]
    start(gather_first())

    half = jnp.where(lax.broadcasted_iota(jnp.int32, (8, 128), 1) >= 64, 4.0, 0.0)
    half = jnp.where(lax.broadcasted_iota(jnp.int32, (8, 128), 0) < 4, half, 0.0)

    def sort(q, carry):
        slots = lax.broadcasted_iota(jnp.int32, (256, POINTS), 0) + q * 256
        place = (slots == jnp.broadcast_to(srow[...], (256, POINTS))).astype(F32).astype(BF16)
        out = lax.dot_general(lhs[...], place, TRANSPOSED, preferred_element_type=F32)
        for xx in range(NX):
            for zz in range(2):
                part = out[xx * ROWS:(xx + 1) * ROWS, zz * 128:(zz + 1) * 128]
                sb[xx, pl.ds(2 * q + zz, 80, stride=8), :] = part[:80] + part[80:160]
                lb[xx, pl.ds(2 * q + zz, 8, stride=8), :] = part[160:168] + half
        return carry

    lax.fori_loop(0, 2, sort, 0)
    wait(gather_first())
    qa[pl.ds(pl.multiple_of(x * 24, 8), 24), :] = p0[pl.ds(0, 24), :]
    qb[pl.ds(pl.multiple_of(y * 24, 8), 24), :] = p0[pl.ds(24, 24), :]
    start(gather_second())
    lax.fori_loop(2, 4, sort, 0)
    wait(gather_second())
    ra[pl.ds(pl.multiple_of((core * NY + y) * 96, 8), 96), :] = qa[...]
    rb[pl.ds(pl.multiple_of((x * NC + core) * 96, 8), 96), :] = qb[...]
    start(gather_core())

    def cam_tile(xx, kk, c):
        return sb[xx, pl.ds((kk * 8 + c) * 8, 8), :]

    def spread(xx, zz, dense):
        gs = lax.broadcasted_iota(jnp.int32, (8, 128), 0).astype(F32)
        columns = []
        for k in range(TRACK):
            hit = gs == jnp.broadcast_to(lb[xx, pl.ds(k * 8 + zz, 1), :], (8, 128))
            tiles = []
            for part in range(2):
                for c in range(6):
                    row = vb[pl.ds(((part * TRACK + k) * 6 + c) * 8 + zz, 1), :]
                    tiles.append(jnp.where(hit, jnp.broadcast_to(row, (8, 128)), 0.0))
            columns.append(jnp.concatenate(tiles, axis=0).astype(BF16))
        left = jnp.concatenate(columns, axis=1)
        out = lax.dot_general(left, ohb[xx * 8 + zz], TRANSPOSED, preferred_element_type=F32)
        out = out[:48] + out[48:]
        for c in range(6):
            dense[pl.ds(xx * 384 + c * 8 + zz, 8, stride=48), :] = out[c * 8:c * 8 + 8]

    def hold(k, c, value):
        high = value.astype(BF16).astype(F32)
        vb[pl.ds((k * 6 + c) * 8, 8), :] = high
        vb[pl.ds(((TRACK + k) * 6 + c) * 8, 8), :] = value - high

    def grad_part(xx, carry):
        for k in range(TRACK):
            e0 = sb[xx, pl.ds((72 + 2 * k) * 8, 8), :]
            e1 = sb[xx, pl.ds((73 + 2 * k) * 8, 8), :]
            for c in range(6):
                hold(k, c, cam_tile(xx, 2 * k, c) * e0 + cam_tile(xx, 2 * k + 1, c) * e1)
        locals_of = lax.broadcasted_iota(jnp.int32, (128, 128), 0).astype(F32)
        for zz in range(NZ):
            for k in range(TRACK):
                label = lb[xx, pl.ds((4 + k) * 8 + zz, 1), :]
                ohb[xx * 8 + zz, :, pl.ds(k * 128, 128)] = (
                    locals_of == jnp.broadcast_to(label, (128, 128))
                ).astype(F32).astype(BF16)
            spread(xx, zz, gbuf)
        sum_core(24, gbuf, in1g, xx).start()
        return carry

    lax.fori_loop(0, NX, grad_part, 0)
    wait(gather_core())

    def schur_part(xx, carry):
        for zz in range(NZ):
            for c in range(3):
                tt[zz, pl.ds(c, 8, stride=8), :] = ra[pl.ds(xx * 24 + c * 8 + zz, 8, stride=96), :]
                tt[zz, pl.ds(3 + c, 8, stride=8), :] = (
                    rb[pl.ds(xx * 192 + c * 8 + zz, 8, stride=24), :]
                )
            high, low = split(tt[zz])
            onehot = ohb[xx * 8 + zz]
            got = jnp.dot(
                jnp.concatenate([high, low], axis=1),
                jnp.concatenate([onehot, onehot], axis=0),
                preferred_element_type=F32,
            )
            for k in range(TRACK):
                group = jnp.broadcast_to(lb[xx, pl.ds(k * 8 + zz, 1), :], (8, 128))
                mine = jnp.zeros((8, 128), F32)
                for g in range(8):
                    mine += jnp.where(
                        group == g, got[g * 8:g * 8 + 8, k * 128:(k + 1) * 128], 0.0
                    )
                db[pl.ds(k * 64 + zz, 8, stride=8), :] = mine
        image = []
        for k in range(TRACK):
            for i in range(2):
                image.append(
                    sum(
                        cam_tile(xx, 2 * k + i, c) * db[pl.ds((k * 8 + c) * 8, 8), :]
                        for c in range(6)
                    )
                )

        def point_tile(kk, j):
            at = kk * 8 + 6 + j if j < 2 else 64 + kk
            return sb[xx, pl.ds(at * 8, 8), :]

        through = [sum(point_tile(kk, j) * image[kk] for kk in range(8)) for j in range(3)]
        image = [image[kk] - sum(point_tile(kk, j) * through[j] for j in range(3)) for kk in range(8)]
        for k in range(TRACK):
            for c in range(6):
                hold(
                    k, c,
                    cam_tile(xx, 2 * k, c) * image[2 * k]
                    + cam_tile(xx, 2 * k + 1, c) * image[2 * k + 1],
                )
        for zz in range(NZ):
            spread(xx, zz, sbuf)
        sum_core(47, sbuf, in1s, xx).start()
        return carry

    def advance_first(base, dense, in1, r1a, r1b, in2a, in2b):
        wait([sum_core(base, dense, in1, xx) for xx in range(NX)])
        fold_core(dense, in1, r1a, r1b)
        start(sum_first(base, r1a, r1b, in2a, in2b))

    def advance_second(base, r1a, r1b, in2a, in2b, r2a, r2b, in3a, in3b):
        wait(sum_first(base, r1a, r1b, in2a, in2b))
        r2a[...] = fold(r1a, in2a, x, NX, 96)
        r2b[...] = fold(r1b, in2b, y, NY, 96)
        start(sum_second(base, r2a, r2b, in3a, in3b))

    def advance_z(base, r2a, r2b, in3a, in3b, r3, r4, in4):
        wait(sum_second(base, r2a, r2b, in3a, in3b))
        r3[pl.ds(0, 24), :] = fold(r2a, in3a, y, NY, 24)
        r3[pl.ds(24, 24), :] = fold(r2b, in3b, x, NX, 24)
        for zz in range(NZ):
            r4[pl.ds(zz * 8, 6), :] = r3[pl.ds(zz, 6, stride=8), :]
        start(sum_z(base, r4, in4))

    def finish(base, r4, in4):
        wait(sum_z(base, r4, in4))
        return fold(r4, in4, z, NZ, 8)[:6]

    lax.fori_loop(0, 1, schur_part, 0)
    advance_first(24, gbuf, in1g, r1ag, r1bg, in2ag, in2bg)
    lax.fori_loop(1, 3, schur_part, 0)
    advance_second(24, r1ag, r1bg, in2ag, in2bg, r2ag, r2bg, in3ag, in3bg)
    lax.fori_loop(3, NX, schur_part, 0)
    advance_z(24, r2ag, r2bg, in3ag, in3bg, r3g, r4g, in4g)
    advance_first(47, sbuf, in1s, r1as, r1bs, in2as, in2bs)
    og_ref[...] = finish(24, r4g, in4g)
    advance_second(47, r1as, r1bs, in2as, in2bs, r2as, r2bs, in3as, in3bs)
    advance_z(47, r2as, r2bs, in3as, in3bs, r3s, r4s, in4s)
    os_ref[...] = cdamp_ref[...] * dir_ref[...] + finish(47, r4s, in4s)


def shards(jac_cam, jac_pt, resid, point_damping, cluster, cam_local, direction, cam_damping):
    def buffer(*shape):
        return pltpu.VMEM(shape, F32)

    scratch = [
        buffer(POINTS // 128, 24, 128), buffer(8, POINTS), pltpu.VMEM((1, POINTS), jnp.int32),
        pltpu.VMEM((NX * ROWS, POINTS), BF16),
        buffer(NX, 640, 128), buffer(NX, 64, 128), buffer(256, 128), buffer(384, 128),
        pltpu.VMEM((32, 128, 512), BF16), buffer(8, 64, 128),
        buffer(64, 128), buffer(48, 128), buffer(96, 128), buffer(96, 128),
        buffer(768, 128), buffer(768, 128),
        buffer(1536, 128), buffer(1536, 128), buffer(768, 128), buffer(768, 128),
    ]
    scratch += [buffer(384, 128) for _ in range(8)]
    scratch += [buffer(96, 128) for _ in range(8)]
    scratch += [buffer(48, 128) for _ in range(2)]
    scratch += [buffer(64, 128) for _ in range(4)]
    scratch += [pltpu.SemaphoreType.DMA((70,)), pltpu.SemaphoreType.DMA((70,))]
    whole = pl.BlockSpec(memory_space=pltpu.VMEM)
    shape = jax.ShapeDtypeStruct((6, 128), F32)
    return pl.pallas_call(
        kernel,
        out_shape=(shape, shape),
        in_specs=[whole] * 8,
        out_specs=(whole, whole),
        scratch_shapes=scratch,
        compiler_params=pltpu.CompilerParams(
            collective_id=0, has_side_effects=True, vmem_limit_bytes=48 * 1024 * 1024
        ),
    )(
        jac_cam.reshape(8, 6, POINTS),
        jac_pt.reshape(8, 3, POINTS),
        resid,
        point_damping.reshape(1, POINTS),
        cluster.T,
        cam_local.T,
        direction,
        cam_damping.reshape(1, 128),
    )


def solution(mesh):
    in_specs = (
        P(None, None, None, ("pts", "cam")),
        P(None, None, None, ("pts", "cam")),
        P(None, None, ("pts", "cam")),
        P(("pts", "cam")),
        P(("pts", "cam"), None),
        P(("pts", "cam"), None),
        P(None, ("pts", "cam")),
        P(("pts", "cam")),
    )
    out_specs = (P(None, ("pts", "cam")), P(None, ("pts", "cam")))
    return jax.shard_map(shards, mesh=mesh, in_specs=in_specs, out_specs=out_specs, check_vma=False)
```

```python
import jax
import jax.numpy as jnp
from jax import lax
from jax.experimental import pallas as pl
from jax.experimental.pallas import tpu as pltpu
from jax.sharding import PartitionSpec as P

MESH = pl.DeviceIdType.MESH
F32 = jnp.float32
BF16 = jnp.bfloat16
NX, NY, NZ, NC = 4, 4, 8, 2
POINTS = 2048
CHUNK = 256
ROWS = 176
TRACK = 4
TRANSPOSED = (((1,), (1,)), ((), ()))


def split(value):
    high = value.astype(BF16)
    low = (value - high.astype(F32)).astype(BF16)
    return high, low


def kernel(
    jc_ref, jp_ref, rs_ref, damp_ref, clu_ref, loc_ref, dir_ref, cdamp_ref,
    os_ref,
    at, bt, rt, damp, clu, loc, own, cdamp,
    srow, lhs, sb, lb, db, vb, ohb, tt,
    zb, p0, dirs,
    gbuf, sbuf, in1g, in1s, r1g, r1s, in2g, in2s, r3, r4, in4,
    send, recv, fetch,
):
    me = lax.axis_index("pts")
    y = lax.axis_index("cam")
    core = lax.rem(me, NC)
    z = lax.rem(lax.div(me, NC), NZ)
    x = lax.div(me, NC * NZ)

    def device(xx, yy, zz, cc):
        return {"pts": (xx * NZ + zz) * NC + cc, "cam": yy}

    def step(at, d, size):
        return lax.rem(at + d, size)

    def rows(ref, start, count):
        return ref.at[pl.ds(pl.multiple_of(start, 8), count), :]

    def copy(src, dst, sem, dev):
        return pltpu.make_async_remote_copy(
            src_ref=src, dst_ref=dst, send_sem=send.at[sem], recv_sem=recv.at[sem],
            device_id=dev, device_id_type=MESH,
        )

    barrier = pltpu.get_barrier_semaphore()
    plane = [(r, d) for r in range(NX) for d in range(NY) if r + d > 0]
    peers = [device(x, y, step(z, d, NZ), core) for d in range(1, NZ)]
    peers += [device(step(x, r, NX), step(y, d, NY), z, core) for r, d in plane]
    peers += [device(x, y, z, 1 - core)]
    for dev in peers:
        pl.semaphore_signal(barrier, inc=1, device_id=dev, device_id_type=MESH)

    fetches = [(dir_ref, own), (clu_ref, clu), (loc_ref, loc), (damp_ref, damp), (cdamp_ref, cdamp)]
    fetches += [(rs_ref.at[k], rt.at[pl.ds(2 * k, 2), :]) for k in range(TRACK)]
    fetches += [
        (jp_ref.at[k, j], bt.at[pl.ds(8 * j + 2 * k, 2), :]) for k in range(TRACK) for j in range(3)
    ]
    fetches += [
        (jc_ref.at[k, c], at.at[pl.ds((k * 6 + c) * 2, 2), :]) for k in range(TRACK) for c in range(6)
    ]
    fetches = [
        pltpu.make_async_copy(src, dst, fetch.at[i]) for i, (src, dst) in enumerate(fetches)
    ]
    for item in fetches:
        item.start()
    tt[...] = jnp.zeros_like(tt)
    r4[...] = jnp.zeros_like(r4)

    def gather_z():
        return [
            copy(own, rows(zb, z * 8, 6), d - 1, device(x, y, step(z, d, NZ), core))
            for d in range(1, NZ)
        ]

    def gather_plane(r, d):
        there = device(step(x, r, NX), step(y, d, NY), z, core)
        return copy(p0, rows(dirs, ((x * NC + core) * NY + y) * 48, 48), 8 + r * NY + d, there)

    def gather_core(i, xx):
        part = rows(dirs, (xx * NC + core) * 192, 192)
        return copy(part, part, 24 + i, device(x, y, z, 1 - core))

    def sum_core(base, dense, in1, i, xx):
        return copy(
            rows(dense, (xx * NC + 1 - core) * 192, 192), rows(in1, xx * 192, 192),
            base + i, device(x, y, z, 1 - core),
        )

    def sum_plane(base, r1, in2, r, d):
        xx, yy = step(x, r, NX), step(y, d, NY)
        return copy(
            rows(r1, (xx * NY + yy) * 48, 48), rows(in2, (x * NY + y) * 48, 48),
            base + r * NY + d, device(xx, yy, z, core),
        )

    def sum_z():
        return [
            copy(rows(r4, step(z, d, NZ) * 16, 16), rows(in4, z * 16, 16), 68 + d,
                 device(x, y, step(z, d, NZ), core))
            for d in range(1, NZ)
        ]

    def turn(i):
        return i + i // 2 - 2 * (i // 3)

    fetches[0].wait()
    pl.semaphore_wait(barrier, len(peers))
    for item in gather_z():
        item.start()
    for item in fetches[1:]:
        item.wait()

    lane = lax.broadcasted_iota(jnp.int32, (CHUNK, CHUNK + 128), 1)
    before = (
        (lax.broadcasted_iota(jnp.int32, (CHUNK, CHUNK + 128), 0) < lane) | (lane >= CHUNK)
    ).astype(F32).astype(BF16)

    def eliminate(b, seen):
        here = pl.ds(pl.multiple_of(b * CHUNK, CHUNK), CHUNK)
        cluster = clu[:, here]
        member = (
            lax.broadcasted_iota(jnp.int32, (64, CHUNK), 0) == jnp.broadcast_to(cluster, (64, CHUNK))
        ).astype(F32)
        counts = jnp.dot(member.astype(BF16), before, preferred_element_type=F32)
        ahead = counts[:, :CHUNK] + jnp.concatenate([seen, seen], axis=1)
        position = jnp.sum(member * ahead, axis=0, keepdims=True)
        slot = jnp.bitwise_and(cluster, 15) * 64 + position.astype(jnp.int32)
        srow[:, here] = slot
        quarter = lax.shift_right_logical(cluster, 4)

        b0, b1, b2 = (bt[pl.ds(8 * j, 8), here] for j in range(3))
        res = rt[:, here]

        def total(value):
            return jnp.sum(value, axis=0, keepdims=True)

        extra = damp[:, here]
        n00, n10, n20 = total(b0 * b0) + extra, total(b1 * b0), total(b2 * b0)
        n11, n21, n22 = total(b1 * b1) + extra, total(b2 * b1), total(b2 * b2) + extra
        q0, q1, q2 = total(b0 * res), total(b1 * res), total(b2 * res)
        ia = 1.0 / jnp.sqrt(n00)
        ba, ca = n10 * ia, n20 * ia
        ib = 1.0 / jnp.sqrt(n11 - ba * ba)
        cb = (n21 - ca * ba) * ib
        ic = 1.0 / jnp.sqrt(n22 - ca * ca - cb * cb)
        c0 = b0 * ia
        c1 = (b1 - ba * c0) * ib
        c2 = (b2 - ca * c0 - cb * c1) * ic
        s0 = q0 * ia
        s1 = (q1 - ba * s0) * ib
        s2 = (q2 - ca * s0 - cb * s1) * ic
        rest = res - (c0 * s0 + c1 * s1 + c2 * s2)

        masks = [
            jnp.broadcast_to((quarter == f).astype(F32), (16, CHUNK)).astype(BF16)
            for f in range(NX)
        ]

        def put(base, value):
            for f in range(NX):
                lhs[pl.ds(f * ROWS + base, 16), here] = value * masks[f]

        for base in range(0, 48, 16):
            high, low = split(at[pl.ds(base, 16), here])
            put(base, high)
            put(80 + base, low)
        for base, pair in ((48, (c0, c1)), (64, (c2, rest))):
            high, low = split(jnp.concatenate(pair, axis=0))
            put(base, high)
            put(80 + base, low)
        label = loc[:, here]
        parts = [
            lax.shift_right_logical(label, 7).astype(F32),
            jnp.bitwise_and(label, 127).astype(F32),
            jnp.zeros((8, CHUNK), F32),
        ]
        put(160, jnp.concatenate(parts, axis=0).astype(BF16))
        return seen + counts[:, CHUNK:]

    lax.fori_loop(0, POINTS // CHUNK, eliminate, jnp.zeros((64, 128), F32))

    half = jnp.where(lax.broadcasted_iota(jnp.int32, (8, 128), 1) >= 64, 4.0, 0.0)
    half = jnp.where(lax.broadcasted_iota(jnp.int32, (8, 128), 0) < 4, half, 0.0)

    def sort(q, carry):
        slots = lax.broadcasted_iota(jnp.int32, (256, POINTS), 0) + q * 256
        place = (slots == jnp.broadcast_to(srow[...], (256, POINTS))).astype(F32).astype(BF16)
        out = lax.dot_general(lhs[...], place, TRANSPOSED, preferred_element_type=F32)
        for xx in range(NX):
            for zz in range(2):
                part = out[xx * ROWS:(xx + 1) * ROWS, zz * 128:(zz + 1) * 128]
                sb[xx, pl.ds(2 * q + zz, 80, stride=8), :] = part[:80] + part[80:160]
                lb[xx, pl.ds(2 * q + zz, 8, stride=8), :] = part[160:168] + half
        return carry

    lax.fori_loop(0, 2, sort, 0)
    for item in gather_z():
        item.wait()
    zb[pl.ds(pl.multiple_of(z * 8, 8), 6), :] = own[...]
    for zz in range(NZ):
        p0[pl.ds(zz, 6, stride=8), :] = zb[pl.ds(zz * 8, 6), :]
    for r, d in plane:
        gather_plane(r, d).start()
    dirs[pl.ds(pl.multiple_of(((x * NC + core) * NY + y) * 48, 8), 48), :] = p0[...]
    lax.fori_loop(2, 4, sort, 0)

    def cam_tile(xx, kk, c):
        return sb[xx, pl.ds(((kk // 2 * 6 + c) * 2 + kk % 2) * 8, 8), :]

    def spread(xx, zz, dense):
        gs = lax.broadcasted_iota(jnp.int32, (8, 128), 0).astype(F32)
        columns = []
        for k in range(TRACK):
            hit = gs == jnp.broadcast_to(lb[xx, pl.ds(k * 8 + zz, 1), :], (8, 128))
            tiles = []
            for part in range(2):
                for c in range(6):
                    row = vb[pl.ds(((part * TRACK + k) * 6 + c) * 8 + zz, 1), :]
                    tiles.append(jnp.where(hit, jnp.broadcast_to(row, (8, 128)), 0.0))
            columns.append(jnp.concatenate(tiles, axis=0).astype(BF16))
        left = jnp.concatenate(columns, axis=1)
        out = lax.dot_general(left, ohb[xx * 8 + zz], TRANSPOSED, preferred_element_type=F32)
        out = out[:48] + out[48:]
        for c in range(6):
            dense[pl.ds(xx * 384 + c * 8 + zz, 8, stride=48), :] = out[c * 8:c * 8 + 8]

    def hold(k, c, value):
        high = value.astype(BF16).astype(F32)
        vb[pl.ds((k * 6 + c) * 8, 8), :] = high
        vb[pl.ds(((TRACK + k) * 6 + c) * 8, 8), :] = value - high

    def grad_part(i, carry):
        xx = step(x, turn(i), NX)
        for k in range(TRACK):
            e0 = sb[xx, pl.ds((72 + 2 * k) * 8, 8), :]
            e1 = sb[xx, pl.ds((73 + 2 * k) * 8, 8), :]
            for c in range(6):
                hold(k, c, cam_tile(xx, 2 * k, c) * e0 + cam_tile(xx, 2 * k + 1, c) * e1)
        locals_of = lax.broadcasted_iota(jnp.int32, (128, 128), 0).astype(F32)
        for zz in range(NZ):
            for k in range(TRACK):
                label = lb[xx, pl.ds((4 + k) * 8 + zz, 1), :]
                ohb[xx * 8 + zz, :, pl.ds(k * 128, 128)] = (
                    locals_of == jnp.broadcast_to(label, (128, 128))
                ).astype(F32).astype(BF16)
            spread(xx, zz, gbuf)
        sum_core(28, gbuf, in1g, i, xx).start()
        return carry

    def schur(xx):
        for zz in range(NZ):
            for c in range(6):
                tt[zz, pl.ds(c, 8, stride=8), :] = dirs[pl.ds(xx * 384 + c * 8 + zz, 8, stride=48), :]
            high, low = split(tt[zz])
            onehot = ohb[xx * 8 + zz]
            got = jnp.dot(
                jnp.concatenate([high, low], axis=1),
                jnp.concatenate([onehot, onehot], axis=0),
                preferred_element_type=F32,
            )
            for k in range(TRACK):
                group = jnp.broadcast_to(lb[xx, pl.ds(k * 8 + zz, 1), :], (8, 128))
                mine = jnp.zeros((8, 128), F32)
                for g in range(8):
                    mine += jnp.where(
                        group == g, got[g * 8:g * 8 + 8, k * 128:(k + 1) * 128], 0.0
                    )
                db[pl.ds(k * 64 + zz, 8, stride=8), :] = mine
        image = []
        for k in range(TRACK):
            for i in range(2):
                image.append(
                    sum(
                        cam_tile(xx, 2 * k + i, c) * db[pl.ds((k * 8 + c) * 8, 8), :]
                        for c in range(6)
                    )
                )

        def point_tile(kk, j):
            return sb[xx, pl.ds((48 + j * 8 + kk) * 8, 8), :]

        through = [sum(point_tile(kk, j) * image[kk] for kk in range(8)) for j in range(3)]
        image = [image[kk] - sum(point_tile(kk, j) * through[j] for j in range(3)) for kk in range(8)]
        for k in range(TRACK):
            for c in range(6):
                hold(
                    k, c,
                    cam_tile(xx, 2 * k, c) * image[2 * k]
                    + cam_tile(xx, 2 * k + 1, c) * image[2 * k + 1],
                )
        for zz in range(NZ):
            spread(xx, zz, sbuf)

    lax.fori_loop(0, NX, grad_part, 0)

    def pass_on(i):
        r = turn(i)
        xx = step(x, r, NX)
        for d in range(NY):
            sent = 8 + lax.rem(NX - r, NX) * NY + (NY - d) % NY
            yy = step(y, d, NY)
            part = rows(dirs, ((xx * NC + core) * NY + yy) * 48, 48)

            def arrive():
                copy(p0, part, sent, device(xx, yy, z, core)).wait_recv()

            if d == 0:
                pl.when(i > 0)(arrive)
            else:
                arrive()
        gather_core(i, xx).start()

    def send_blocks(base1, base2, dense, in1, r1, in2, i):
        r = turn(i)
        xx = step(x, r, NX)
        sum_core(base1, dense, in1, i, xx).wait()
        here = pl.ds(pl.multiple_of(xx * 192, 8), 192)
        r1[here, :] = dense[pl.ds(pl.multiple_of((xx * NC + core) * 192, 8), 192), :] + in1[here, :]
        for d in range(NY):
            item = sum_plane(base2, r1, in2, r, d)
            if d == 0:
                pl.when(i > 0)(item.start)
            else:
                item.start()

    def schur_part(i, carry):
        xx = step(x, turn(i), NX)

        @pl.when(i < NX - 1)
        def _():
            pass_on(i + 1)

        send_blocks(28, 36, gbuf, in1g, r1g, in2g, i)
        gather_core(i, xx).wait()
        schur(xx)
        sum_core(32, sbuf, in1s, i, xx).start()

        @pl.when(i > 0)
        def _():
            send_blocks(32, 52, sbuf, in1s, r1s, in2s, i - 1)

        return carry

    pass_on(0)
    lax.fori_loop(0, NX, schur_part, 0)
    send_blocks(32, 52, sbuf, in1s, r1s, in2s, NX - 1)

    def fold_plane(base, r1, in2):
        total = r1[pl.ds(pl.multiple_of((x * NY + y) * 48, 8), 48), :]
        for r, d in plane:
            sum_plane(base, r1, in2, r, d).wait()
            source = step(x, NX - r, NX) * NY + step(y, NY - d, NY)
            total += in2[pl.ds(pl.multiple_of(source * 48, 8), 48), :]
        return total

    for part, total in enumerate((fold_plane(36, r1g, in2g), fold_plane(52, r1s, in2s))):
        r3[...] = total
        for zz in range(NZ):
            r4[pl.ds(zz * 16 + 8 * part, 6), :] = r3[pl.ds(zz, 6, stride=8), :]
    for item in sum_z():
        item.start()
    total = r4[pl.ds(pl.multiple_of(z * 16, 8), 16), :]
    for d, item in enumerate(sum_z()):
        item.wait()
        total += in4[pl.ds(pl.multiple_of(step(z, NZ - 1 - d, NZ) * 16, 8), 16), :]
    for r, d in plane:
        gather_plane(r, d).wait_send()
    os_ref[...] = total


def shards(jac_cam, jac_pt, resid, point_damping, cluster, cam_local, direction, cam_damping):
    def buffer(*shape):
        return pltpu.VMEM(shape, F32)

    scratch = [
        buffer(48, POINTS), buffer(24, POINTS), buffer(8, POINTS), buffer(1, POINTS),
        pltpu.VMEM((1, POINTS), jnp.int32), pltpu.VMEM((TRACK, POINTS), jnp.int32),
        buffer(6, 128), buffer(1, 128),
        pltpu.VMEM((1, POINTS), jnp.int32), pltpu.VMEM((NX * ROWS, POINTS), BF16),
        buffer(NX, 640, 128), buffer(NX, 64, 128), buffer(256, 128), buffer(384, 128),
        pltpu.VMEM((32, 128, 512), BF16), buffer(8, 64, 128),
        buffer(64, 128), buffer(48, 128), buffer(1536, 128),
        buffer(1536, 128), buffer(1536, 128), buffer(768, 128), buffer(768, 128),
        buffer(768, 128), buffer(768, 128), buffer(768, 128), buffer(768, 128),
        buffer(48, 128), buffer(128, 128), buffer(128, 128),
        pltpu.SemaphoreType.DMA((76,)), pltpu.SemaphoreType.DMA((76,)),
        pltpu.SemaphoreType.DMA((45,)),
    ]
    whole = pl.BlockSpec(memory_space=pltpu.VMEM)
    shape = jax.ShapeDtypeStruct((6, 128), F32)
    both = pl.pallas_call(
        kernel,
        out_shape=jax.ShapeDtypeStruct((16, 128), F32),
        in_specs=[pl.BlockSpec(memory_space=pltpu.HBM)] * 8,
        out_specs=whole,
        scratch_shapes=scratch,
        compiler_params=pltpu.CompilerParams(
            collective_id=0, has_side_effects=True, vmem_limit_bytes=62 * 1024 * 1024
        ),
    )(
        jnp.transpose(jac_cam, (0, 2, 1, 3)),
        jnp.transpose(jac_pt, (0, 2, 1, 3)),
        resid,
        point_damping.reshape(1, POINTS),
        cluster.T,
        cam_local.T,
        direction,
        cam_damping.reshape(1, 128),
    )
    return both[:6], cam_damping[None, :] * direction + both[8:14]


def solution(mesh):
    in_specs = (
        P(None, None, None, ("pts", "cam")),
        P(None, None, None, ("pts", "cam")),
        P(None, None, ("pts", "cam")),
        P(("pts", "cam")),
        P(("pts", "cam"), None),
        P(("pts", "cam"), None),
        P(None, ("pts", "cam")),
        P(("pts", "cam")),
    )
    out_specs = (P(None, ("pts", "cam")), P(None, ("pts", "cam")))
    return jax.shard_map(shards, mesh=mesh, in_specs=in_specs, out_specs=out_specs, check_vma=False)
```

```python
import jax
import jax.numpy as jnp
from jax import lax
from jax.experimental import pallas as pl
from jax.experimental.pallas import tpu as pltpu
from jax.sharding import PartitionSpec as P

MESH = pl.DeviceIdType.MESH
F32 = jnp.float32
BF16 = jnp.bfloat16
NX, NY, NZ, NC = 4, 4, 8, 2
POINTS = 2048
CHUNK = 256
ROWS = 176
TRACK = 4
TRANSPOSED = (((1,), (1,)), ((), ()))


def split(value):
    high = value.astype(BF16)
    low = (value - high.astype(F32)).astype(BF16)
    return high, low


def kernel(
    jc_ref, jp_ref, rs_ref, damp_ref, clu_ref, loc_ref, dir_ref, cdamp_ref,
    os_ref,
    at, bt, rt, damp, clu, loc, own, cdamp,
    srow, lhs, sb, lb, db, vb, ohb, tt,
    zb, p0, dirs,
    gbuf, sbuf, in1g, in1s, r1g, r1s, in2g, in2s, r3, r4, in4,
    send, recv, fetch,
):
    me = lax.axis_index("pts")
    y = lax.axis_index("cam")
    core = lax.rem(me, NC)
    z = lax.rem(lax.div(me, NC), NZ)
    x = lax.div(me, NC * NZ)

    def device(xx, yy, zz, cc):
        return {"pts": (xx * NZ + zz) * NC + cc, "cam": yy}

    def step(at, d, size):
        return lax.rem(at + d, size)

    def rows(ref, start, count):
        return ref.at[pl.ds(pl.multiple_of(start, 8), count), :]

    def copy(src, dst, sem, dev):
        return pltpu.make_async_remote_copy(
            src_ref=src, dst_ref=dst, send_sem=send.at[sem], recv_sem=recv.at[sem],
            device_id=dev, device_id_type=MESH,
        )

    barrier = pltpu.get_barrier_semaphore()
    plane = [(r, d) for r in range(NX) for d in range(NY) if r + d > 0]
    peers = [device(x, y, step(z, d, NZ), core) for d in range(1, NZ)]
    peers += [device(step(x, r, NX), step(y, d, NY), z, core) for r, d in plane]
    peers += [device(x, y, z, 1 - core)]
    for dev in peers:
        pl.semaphore_signal(barrier, inc=1, device_id=dev, device_id_type=MESH)

    fetches = [(dir_ref, own), (clu_ref, clu), (loc_ref, loc), (damp_ref, damp), (cdamp_ref, cdamp)]
    fetches += [(rs_ref.at[k], rt.at[pl.ds(2 * k, 2), :]) for k in range(TRACK)]
    fetches += [
        (jp_ref.at[k, j], bt.at[pl.ds(8 * j + 2 * k, 2), :]) for k in range(TRACK) for j in range(3)
    ]
    fetches += [
        (jc_ref.at[k, c], at.at[pl.ds((k * 6 + c) * 2, 2), :]) for k in range(TRACK) for c in range(6)
    ]
    fetches = [
        pltpu.make_async_copy(src, dst, fetch.at[i]) for i, (src, dst) in enumerate(fetches)
    ]
    for item in fetches:
        item.start()
    tt[...] = jnp.zeros_like(tt)
    r4[...] = jnp.zeros_like(r4)

    def gather_z():
        return [
            copy(dir_ref, rows(zb, z * 8, 6), d - 1, device(x, y, step(z, d, NZ), core))
            for d in (4, 3, 5, 2, 6, 1, 7)
        ]

    def gather_plane(r, d):
        there = device(step(x, r, NX), step(y, d, NY), z, core)
        return copy(p0, rows(dirs, ((x * NC + core) * NY + y) * 48, 48), 8 + r * NY + d, there)

    def gather_core(i, xx):
        part = rows(dirs, (xx * NC + core) * 192, 192)
        return copy(part, part, 24 + i, device(x, y, z, 1 - core))

    def sum_core(base, dense, in1, i, xx):
        return copy(
            rows(dense, (xx * NC + 1 - core) * 192, 192), rows(in1, xx * 192, 192),
            base + i, device(x, y, z, 1 - core),
        )

    def sum_plane(base, r1, in2, r, d):
        xx, yy = step(x, r, NX), step(y, d, NY)
        return copy(
            rows(r1, (xx * NY + yy) * 48, 48), rows(in2, (x * NY + y) * 48, 48),
            base + r * NY + d, device(xx, yy, z, core),
        )

    def sum_z():
        return [
            copy(rows(r4, step(z, d, NZ) * 16, 16), rows(in4, z * 16, 16), 68 + d,
                 device(x, y, step(z, d, NZ), core))
            for d in (4, 3, 5, 2, 6, 1, 7)
        ]

    def turn(i):
        return i + i // 2 - 2 * (i // 3)

    pl.semaphore_wait(barrier, len(peers))
    for item in gather_z():
        item.start()
    for item in fetches:
        item.wait()

    lane = lax.broadcasted_iota(jnp.int32, (CHUNK, CHUNK + 128), 1)
    before = (
        (lax.broadcasted_iota(jnp.int32, (CHUNK, CHUNK + 128), 0) < lane) | (lane >= CHUNK)
    ).astype(F32).astype(BF16)

    def eliminate(b, seen):
        here = pl.ds(pl.multiple_of(b * CHUNK, CHUNK), CHUNK)
        cluster = clu[:, here]
        member = (
            lax.broadcasted_iota(jnp.int32, (64, CHUNK), 0) == jnp.broadcast_to(cluster, (64, CHUNK))
        ).astype(F32)
        counts = jnp.dot(member.astype(BF16), before, preferred_element_type=F32)
        ahead = counts[:, :CHUNK] + jnp.concatenate([seen, seen], axis=1)
        position = jnp.sum(member * ahead, axis=0, keepdims=True)
        slot = jnp.bitwise_and(cluster, 15) * 64 + position.astype(jnp.int32)
        srow[:, here] = slot
        quarter = lax.shift_right_logical(cluster, 4)

        b0, b1, b2 = (bt[pl.ds(8 * j, 8), here] for j in range(3))
        res = rt[:, here]

        def total(value):
            return jnp.sum(value, axis=0, keepdims=True)

        extra = damp[:, here]
        n00, n10, n20 = total(b0 * b0) + extra, total(b1 * b0), total(b2 * b0)
        n11, n21, n22 = total(b1 * b1) + extra, total(b2 * b1), total(b2 * b2) + extra
        q0, q1, q2 = total(b0 * res), total(b1 * res), total(b2 * res)
        ia = 1.0 / jnp.sqrt(n00)
        ba, ca = n10 * ia, n20 * ia
        ib = 1.0 / jnp.sqrt(n11 - ba * ba)
        cb = (n21 - ca * ba) * ib
        ic = 1.0 / jnp.sqrt(n22 - ca * ca - cb * cb)
        c0 = b0 * ia
        c1 = (b1 - ba * c0) * ib
        c2 = (b2 - ca * c0 - cb * c1) * ic
        s0 = q0 * ia
        s1 = (q1 - ba * s0) * ib
        s2 = (q2 - ca * s0 - cb * s1) * ic
        rest = res - (c0 * s0 + c1 * s1 + c2 * s2)

        masks = [
            jnp.broadcast_to((quarter == f).astype(F32), (16, CHUNK)).astype(BF16)
            for f in range(NX)
        ]

        def put(base, value):
            for f in range(NX):
                lhs[pl.ds(f * ROWS + base, 16), here] = value * masks[f]

        for base in range(0, 48, 16):
            high, low = split(at[pl.ds(base, 16), here])
            put(base, high)
            put(80 + base, low)
        for base, pair in ((48, (c0, c1)), (64, (c2, rest))):
            high, low = split(jnp.concatenate(pair, axis=0))
            put(base, high)
            put(80 + base, low)
        label = loc[:, here]
        parts = [
            lax.shift_right_logical(label, 7).astype(F32),
            jnp.bitwise_and(label, 127).astype(F32),
            jnp.zeros((8, CHUNK), F32),
        ]
        put(160, jnp.concatenate(parts, axis=0).astype(BF16))
        return seen + counts[:, CHUNK:]

    lax.fori_loop(0, POINTS // CHUNK, eliminate, jnp.zeros((64, 128), F32))

    half = jnp.where(lax.broadcasted_iota(jnp.int32, (8, 128), 1) >= 64, 4.0, 0.0)
    half = jnp.where(lax.broadcasted_iota(jnp.int32, (8, 128), 0) < 4, half, 0.0)

    def sort(q, carry):
        slots = lax.broadcasted_iota(jnp.int32, (256, POINTS), 0) + q * 256
        place = (slots == jnp.broadcast_to(srow[...], (256, POINTS))).astype(F32).astype(BF16)
        out = lax.dot_general(lhs[...], place, TRANSPOSED, preferred_element_type=F32)
        for xx in range(NX):
            for zz in range(2):
                part = out[xx * ROWS:(xx + 1) * ROWS, zz * 128:(zz + 1) * 128]
                sb[xx, pl.ds(2 * q + zz, 80, stride=8), :] = part[:80] + part[80:160]
                lb[xx, pl.ds(2 * q + zz, 8, stride=8), :] = part[160:168] + half
        return carry

    lax.fori_loop(0, 2, sort, 0)
    for item in gather_z():
        item.wait()
    zb[pl.ds(pl.multiple_of(z * 8, 8), 6), :] = own[...]
    for zz in range(NZ):
        p0[pl.ds(zz, 6, stride=8), :] = zb[pl.ds(zz * 8, 6), :]
    for r in (0, 1, 3, 2):
        for d in (2, 1, 3, 0):
            if r + d > 0:
                gather_plane(r, d).start()
    dirs[pl.ds(pl.multiple_of(((x * NC + core) * NY + y) * 48, 8), 48), :] = p0[...]
    lax.fori_loop(2, 4, sort, 0)

    def cam_tile(xx, kk, c):
        return sb[xx, pl.ds(((kk // 2 * 6 + c) * 2 + kk % 2) * 8, 8), :]

    def spread(xx, zz, dense):
        gs = lax.broadcasted_iota(jnp.int32, (8, 128), 0).astype(F32)
        columns = []
        for k in range(TRACK):
            hit = gs == jnp.broadcast_to(lb[xx, pl.ds(k * 8 + zz, 1), :], (8, 128))
            tiles = []
            for part in range(2):
                for c in range(6):
                    row = vb[pl.ds(((part * TRACK + k) * 6 + c) * 8 + zz, 1), :]
                    tiles.append(jnp.where(hit, jnp.broadcast_to(row, (8, 128)), 0.0))
            columns.append(jnp.concatenate(tiles, axis=0).astype(BF16))
        left = jnp.concatenate(columns, axis=1)
        out = lax.dot_general(left, ohb[xx * 8 + zz], TRANSPOSED, preferred_element_type=F32)
        out = out[:48] + out[48:]
        for c in range(6):
            dense[pl.ds(xx * 384 + c * 8 + zz, 8, stride=48), :] = out[c * 8:c * 8 + 8]

    def hold(k, c, value):
        high = value.astype(BF16).astype(F32)
        vb[pl.ds((k * 6 + c) * 8, 8), :] = high
        vb[pl.ds(((TRACK + k) * 6 + c) * 8, 8), :] = value - high

    def grad_part(i, carry):
        xx = step(x, turn(i), NX)
        for k in range(TRACK):
            e0 = sb[xx, pl.ds((72 + 2 * k) * 8, 8), :]
            e1 = sb[xx, pl.ds((73 + 2 * k) * 8, 8), :]
            for c in range(6):
                hold(k, c, cam_tile(xx, 2 * k, c) * e0 + cam_tile(xx, 2 * k + 1, c) * e1)
        locals_of = lax.broadcasted_iota(jnp.int32, (128, 128), 0).astype(F32)
        for zz in range(NZ):
            for k in range(TRACK):
                label = lb[xx, pl.ds((4 + k) * 8 + zz, 1), :]
                ohb[xx * 8 + zz, :, pl.ds(k * 128, 128)] = (
                    locals_of == jnp.broadcast_to(label, (128, 128))
                ).astype(F32).astype(BF16)
            spread(xx, zz, gbuf)
        sum_core(28, gbuf, in1g, i, xx).start()
        return carry

    def schur(xx):
        for zz in range(NZ):
            for c in range(6):
                tt[zz, pl.ds(c, 8, stride=8), :] = dirs[pl.ds(xx * 384 + c * 8 + zz, 8, stride=48), :]
            high, low = split(tt[zz])
            onehot = ohb[xx * 8 + zz]
            got = jnp.dot(
                jnp.concatenate([high, low], axis=1),
                jnp.concatenate([onehot, onehot], axis=0),
                preferred_element_type=F32,
            )
            for k in range(TRACK):
                group = jnp.broadcast_to(lb[xx, pl.ds(k * 8 + zz, 1), :], (8, 128))
                mine = jnp.zeros((8, 128), F32)
                for g in range(8):
                    mine += jnp.where(
                        group == g, got[g * 8:g * 8 + 8, k * 128:(k + 1) * 128], 0.0
                    )
                db[pl.ds(k * 64 + zz, 8, stride=8), :] = mine
        image = []
        for k in range(TRACK):
            for i in range(2):
                image.append(
                    sum(
                        cam_tile(xx, 2 * k + i, c) * db[pl.ds((k * 8 + c) * 8, 8), :]
                        for c in range(6)
                    )
                )

        def point_tile(kk, j):
            return sb[xx, pl.ds((48 + j * 8 + kk) * 8, 8), :]

        through = [sum(point_tile(kk, j) * image[kk] for kk in range(8)) for j in range(3)]
        image = [image[kk] - sum(point_tile(kk, j) * through[j] for j in range(3)) for kk in range(8)]
        for k in range(TRACK):
            for c in range(6):
                hold(
                    k, c,
                    cam_tile(xx, 2 * k, c) * image[2 * k]
                    + cam_tile(xx, 2 * k + 1, c) * image[2 * k + 1],
                )
        for zz in range(NZ):
            spread(xx, zz, sbuf)

    lax.fori_loop(0, NX, grad_part, 0)

    def own_group():
        for d in range(1, NY):
            part = rows(dirs, ((x * NC + core) * NY + step(y, d, NY)) * 48, 48)
            copy(p0, part, 8 + NY - d, device(x, step(y, d, NY), z, core)).wait_recv()
        gather_core(0, x).start()

    def pass_on(i):
        r = turn(i)
        xx = step(x, r, NX)
        for d in range(NY):
            sent = 8 + (NX - r) * NY + (NY - d) % NY
            yy = step(y, d, NY)
            part = rows(dirs, ((xx * NC + core) * NY + yy) * 48, 48)
            copy(p0, part, sent, device(xx, yy, z, core)).wait_recv()
        gather_core(i, xx).start()

    def send_blocks(base1, base2, dense, in1, r1, in2, i):
        r = turn(i)
        xx = step(x, r, NX)
        sum_core(base1, dense, in1, i, xx).wait()
        here = pl.ds(pl.multiple_of(xx * 192, 8), 192)
        r1[here, :] = dense[pl.ds(pl.multiple_of((xx * NC + core) * 192, 8), 192), :] + in1[here, :]
        for d in (2, 1, 3, 0):
            item = sum_plane(base2, r1, in2, r, d)
            if d == 0:
                pl.when(i > 0)(item.start)
            else:
                item.start()

    def schur_part(i, carry):
        xx = step(x, turn(i), NX)

        @pl.when(i < 2)
        def _():
            pass_on(i + 2)

        gather_core(i, xx).wait()

        schur(xx)

        sum_core(32, sbuf, in1s, i, xx).start()

        @pl.when(i >= 2)
        def _():
            send_blocks(32, 52, sbuf, in1s, r1s, in2s, i - 2)

        return carry

    def send_grad(i, carry):
        send_blocks(28, 36, gbuf, in1g, r1g, in2g, i)
        return carry

    own_group()
    pass_on(1)
    lax.fori_loop(0, NX, send_grad, 0)
    lax.fori_loop(0, NX, schur_part, 0)
    send_blocks(32, 52, sbuf, in1s, r1s, in2s, 2)
    send_blocks(32, 52, sbuf, in1s, r1s, in2s, 3)

    def block(at):
        return pl.ds(pl.multiple_of(at * 48, 8), 48)

    def from_source(r, d):
        return block(step(x, NX - r, NX) * NY + step(y, NY - d, NY))

    def fold_grad():
        total = r1g[block(x * NY + y), :]
        for r, d in plane:
            sum_plane(36, r1g, in2g, r, d).wait()
            total += in2g[from_source(r, d), :]
        return total

    def fold_prod():
        total = r1s[block(x * NY + y), :]
        for r in (0, 1, 3, 2):
            for d in range(NY):
                if r + d > 0:
                    sum_plane(52, r1s, in2s, r, d).wait()
                    total += in2s[from_source(r, d), :]
        return total

    for part, total in enumerate((fold_grad(), fold_prod())):
        r3[...] = total
        for zz in range(NZ):
            r4[pl.ds(zz * 16 + 8 * part, 6), :] = r3[pl.ds(zz, 6, stride=8), :]
    for item in sum_z():
        item.start()
    total = r4[pl.ds(pl.multiple_of(z * 16, 8), 16), :]
    for item in sum_z():
        item.wait()
    for d in range(1, NZ):
        total += in4[pl.ds(pl.multiple_of(step(z, d, NZ) * 16, 8), 16), :]
    for r, d in plane:
        gather_plane(r, d).wait_send()
    os_ref[...] = total


def shards(jac_cam, jac_pt, resid, point_damping, cluster, cam_local, direction, cam_damping):
    def buffer(*shape):
        return pltpu.VMEM(shape, F32)

    scratch = [
        buffer(48, POINTS), buffer(24, POINTS), buffer(8, POINTS), buffer(1, POINTS),
        pltpu.VMEM((1, POINTS), jnp.int32), pltpu.VMEM((TRACK, POINTS), jnp.int32),
        buffer(6, 128), buffer(1, 128),
        pltpu.VMEM((1, POINTS), jnp.int32), pltpu.VMEM((NX * ROWS, POINTS), BF16),
        buffer(NX, 640, 128), buffer(NX, 64, 128), buffer(256, 128), buffer(384, 128),
        pltpu.VMEM((32, 128, 512), BF16), buffer(8, 64, 128),
        buffer(64, 128), buffer(48, 128), buffer(1536, 128),
        buffer(1536, 128), buffer(1536, 128), buffer(768, 128), buffer(768, 128),
        buffer(768, 128), buffer(768, 128), buffer(768, 128), buffer(768, 128),
        buffer(48, 128), buffer(128, 128), buffer(128, 128),
        pltpu.SemaphoreType.DMA((76,)), pltpu.SemaphoreType.DMA((76,)),
        pltpu.SemaphoreType.DMA((45,)),
    ]
    whole = pl.BlockSpec(memory_space=pltpu.VMEM)
    shape = jax.ShapeDtypeStruct((6, 128), F32)
    both = pl.pallas_call(
        kernel,
        out_shape=jax.ShapeDtypeStruct((16, 128), F32),
        in_specs=[pl.BlockSpec(memory_space=pltpu.HBM)] * 8,
        out_specs=whole,
        scratch_shapes=scratch,
        compiler_params=pltpu.CompilerParams(
            collective_id=0, has_side_effects=True, vmem_limit_bytes=62 * 1024 * 1024
        ),
    )(
        jnp.transpose(jac_cam, (0, 2, 1, 3)),
        jnp.transpose(jac_pt, (0, 2, 1, 3)),
        resid,
        point_damping.reshape(1, POINTS),
        cluster.T,
        cam_local.T,
        direction,
        cam_damping.reshape(1, 128),
    )
    return both[:6], cam_damping[None, :] * direction + both[8:14]


def solution(mesh):
    in_specs = (
        P(None, None, None, ("pts", "cam")),
        P(None, None, None, ("pts", "cam")),
        P(None, None, ("pts", "cam")),
        P(("pts", "cam")),
        P(("pts", "cam"), None),
        P(("pts", "cam"), None),
        P(None, ("pts", "cam")),
        P(("pts", "cam")),
    )
    out_specs = (P(None, ("pts", "cam")), P(None, ("pts", "cam")))
    return jax.shard_map(shards, mesh=mesh, in_specs=in_specs, out_specs=out_specs, check_vma=False)
```

```python
import jax
import jax.numpy as jnp
from jax import lax
from jax.experimental import pallas as pl
from jax.experimental.pallas import tpu as pltpu
from jax.sharding import PartitionSpec as P

MESH = pl.DeviceIdType.MESH
F32 = jnp.float32
BF16 = jnp.bfloat16
NX, NY, NZ, NC = 4, 4, 8, 2
POINTS = 2048
CHUNK = 256
ROWS = 176
TRACK = 4
TRANSPOSED = (((1,), (1,)), ((), ()))


def split(value):
    high = value.astype(BF16)
    low = (value - high.astype(F32)).astype(BF16)
    return high, low


def kernel(
    jc_ref, jp_ref, rs_ref, damp_ref, clu_ref, loc_ref, dir_ref, cdamp_ref,
    os_ref,
    at, bt, rt, damp, clu, loc, own, cdamp,
    srow, lhs, sb, lb, db, vb, ohb, tt,
    zb, p0, dirs,
    gbuf, sbuf, in1g, in1s, r1g, r1s, in2g, in2s, r3, r4, in4,
    send, recv, fetch,
):
    me = lax.axis_index("pts")
    y = lax.axis_index("cam")
    core = lax.rem(me, NC)
    z = lax.rem(lax.div(me, NC), NZ)
    x = lax.div(me, NC * NZ)

    def device(xx, yy, zz, cc):
        return {"pts": (xx * NZ + zz) * NC + cc, "cam": yy}

    def step(at, d, size):
        return lax.rem(at + d, size)

    def rows(ref, start, count):
        return ref.at[pl.ds(pl.multiple_of(start, 8), count), :]

    def copy(src, dst, sem, dev):
        return pltpu.make_async_remote_copy(
            src_ref=src, dst_ref=dst, send_sem=send.at[sem], recv_sem=recv.at[sem],
            device_id=dev, device_id_type=MESH,
        )

    barrier = pltpu.get_barrier_semaphore()
    plane = [(r, d) for r in range(NX) for d in range(NY) if r + d > 0]
    peers = [device(x, y, step(z, d, NZ), core) for d in (4, 3, 5)]
    peers += [
        device(step(x, r, NX), step(y, d, NY), z, core)
        for r in (2, 1, 3, 0) for d in (2, 1, 3, 0) if r + d > 0
    ]
    peers += [device(x, y, step(z, d, NZ), core) for d in (2, 6, 1, 7)]
    peers += [device(x, y, z, 1 - core)]
    for dev in peers:
        pl.semaphore_signal(barrier, inc=1, device_id=dev, device_id_type=MESH)

    fetches = [(dir_ref, own), (clu_ref, clu), (loc_ref, loc), (damp_ref, damp), (cdamp_ref, cdamp)]
    fetches += [(rs_ref.at[k], rt.at[pl.ds(2 * k, 2), :]) for k in range(TRACK)]
    fetches += [
        (jp_ref.at[k, j], bt.at[pl.ds(8 * j + 2 * k, 2), :]) for k in range(TRACK) for j in range(3)
    ]
    fetches += [
        (jc_ref.at[k, c], at.at[pl.ds((k * 6 + c) * 2, 2), :]) for k in range(TRACK) for c in range(6)
    ]
    fetches = [
        pltpu.make_async_copy(src, dst, fetch.at[i]) for i, (src, dst) in enumerate(fetches)
    ]
    for item in fetches:
        item.start()
    tt[...] = jnp.zeros_like(tt)
    r4[...] = jnp.zeros_like(r4)

    def gather_z():
        return [
            copy(dir_ref, rows(zb, z * 8, 6), d - 1, device(x, y, step(z, d, NZ), core))
            for d in (4, 3, 5, 2, 6, 1, 7)
        ]

    def gather_plane(r, d):
        there = device(step(x, r, NX), step(y, d, NY), z, core)
        return copy(p0, rows(dirs, ((x * NC + core) * NY + y) * 48, 48), 8 + r * NY + d, there)

    def gather_core(i, xx):
        part = rows(dirs, (xx * NC + core) * 192, 192)
        return copy(part, part, 24 + i, device(x, y, z, 1 - core))

    def sum_core(base, dense, in1, i, xx):
        return copy(
            rows(dense, (xx * NC + 1 - core) * 192, 192), rows(in1, xx * 192, 192),
            base + i, device(x, y, z, 1 - core),
        )

    def sum_plane(base, r1, in2, r, d):
        xx, yy = step(x, r, NX), step(y, d, NY)
        return copy(
            rows(r1, (xx * NY + yy) * 48, 48), rows(in2, (x * NY + y) * 48, 48),
            base + r * NY + d, device(xx, yy, z, core),
        )

    def sum_z():
        return [
            copy(rows(r4, step(z, d, NZ) * 16, 16), rows(in4, z * 16, 16), 68 + d,
                 device(x, y, step(z, d, NZ), core))
            for d in (4, 3, 5, 2, 6, 1, 7)
        ]

    def turn(i):
        return (i + 1) % NX

    pl.semaphore_wait(barrier, len(peers))
    for item in gather_z():
        item.start()
    for item in fetches:
        item.wait()

    lane = lax.broadcasted_iota(jnp.int32, (CHUNK, CHUNK + 128), 1)
    before = (
        (lax.broadcasted_iota(jnp.int32, (CHUNK, CHUNK + 128), 0) < lane) | (lane >= CHUNK)
    ).astype(F32).astype(BF16)

    def eliminate(b, seen):
        here = pl.ds(pl.multiple_of(b * CHUNK, CHUNK), CHUNK)
        cluster = clu[:, here]
        member = (
            lax.broadcasted_iota(jnp.int32, (64, CHUNK), 0) == jnp.broadcast_to(cluster, (64, CHUNK))
        ).astype(F32)
        counts = jnp.dot(member.astype(BF16), before, preferred_element_type=F32)
        ahead = counts[:, :CHUNK] + jnp.concatenate([seen, seen], axis=1)
        position = jnp.sum(member * ahead, axis=0, keepdims=True)
        slot = jnp.bitwise_and(cluster, 15) * 64 + position.astype(jnp.int32)
        srow[:, here] = slot
        quarter = lax.shift_right_logical(cluster, 4)

        b0, b1, b2 = (bt[pl.ds(8 * j, 8), here] for j in range(3))
        res = rt[:, here]

        def total(value):
            return jnp.sum(value, axis=0, keepdims=True)

        extra = damp[:, here]
        n00, n10, n20 = total(b0 * b0) + extra, total(b1 * b0), total(b2 * b0)
        n11, n21, n22 = total(b1 * b1) + extra, total(b2 * b1), total(b2 * b2) + extra
        q0, q1, q2 = total(b0 * res), total(b1 * res), total(b2 * res)
        ia = 1.0 / jnp.sqrt(n00)
        ba, ca = n10 * ia, n20 * ia
        ib = 1.0 / jnp.sqrt(n11 - ba * ba)
        cb = (n21 - ca * ba) * ib
        ic = 1.0 / jnp.sqrt(n22 - ca * ca - cb * cb)
        c0 = b0 * ia
        c1 = (b1 - ba * c0) * ib
        c2 = (b2 - ca * c0 - cb * c1) * ic
        s0 = q0 * ia
        s1 = (q1 - ba * s0) * ib
        s2 = (q2 - ca * s0 - cb * s1) * ic
        rest = res - (c0 * s0 + c1 * s1 + c2 * s2)

        masks = [
            jnp.broadcast_to((quarter == f).astype(F32), (16, CHUNK)).astype(BF16)
            for f in range(NX)
        ]

        def put(base, value):
            for f in range(NX):
                lhs[pl.ds(f * ROWS + base, 16), here] = value * masks[f]

        for base in range(0, 48, 16):
            high, low = split(at[pl.ds(base, 16), here])
            put(base, high)
            put(80 + base, low)
        for base, pair in ((48, (c0, c1)), (64, (c2, rest))):
            high, low = split(jnp.concatenate(pair, axis=0))
            put(base, high)
            put(80 + base, low)
        label = loc[:, here]
        parts = [
            lax.shift_right_logical(label, 7).astype(F32),
            jnp.bitwise_and(label, 127).astype(F32),
            jnp.zeros((8, CHUNK), F32),
        ]
        put(160, jnp.concatenate(parts, axis=0).astype(BF16))
        return seen + counts[:, CHUNK:]

    lax.fori_loop(0, POINTS // CHUNK, eliminate, jnp.zeros((64, 128), F32))

    half = jnp.where(lax.broadcasted_iota(jnp.int32, (8, 128), 1) >= 64, 4.0, 0.0)
    half = jnp.where(lax.broadcasted_iota(jnp.int32, (8, 128), 0) < 4, half, 0.0)

    def sort(q, carry):
        slots = lax.broadcasted_iota(jnp.int32, (256, POINTS), 0) + q * 256
        place = (slots == jnp.broadcast_to(srow[...], (256, POINTS))).astype(F32).astype(BF16)
        out = lax.dot_general(lhs[...], place, TRANSPOSED, preferred_element_type=F32)
        for xx in range(NX):
            for zz in range(2):
                part = out[xx * ROWS:(xx + 1) * ROWS, zz * 128:(zz + 1) * 128]
                sb[xx, pl.ds(2 * q + zz, 80, stride=8), :] = part[:80] + part[80:160]
                lb[xx, pl.ds(2 * q + zz, 8, stride=8), :] = part[160:168] + half
        return carry

    lax.fori_loop(0, 2, sort, 0)
    for item in gather_z():
        item.wait()
    zb[pl.ds(pl.multiple_of(z * 8, 8), 6), :] = own[...]
    for zz in range(NZ):
        p0[pl.ds(zz, 6, stride=8), :] = zb[pl.ds(zz * 8, 6), :]
    for r in (0, 1, 3, 2):
        for d in (2, 1, 3, 0):
            if r + d > 0:
                gather_plane(r, d).start()
    dirs[pl.ds(pl.multiple_of(((x * NC + core) * NY + y) * 48, 8), 48), :] = p0[...]
    lax.fori_loop(2, 4, sort, 0)

    def cam_tile(xx, kk, c):
        return sb[xx, pl.ds(((kk // 2 * 6 + c) * 2 + kk % 2) * 8, 8), :]

    def spread(xx, zz, dense):
        gs = lax.broadcasted_iota(jnp.int32, (8, 128), 0).astype(F32)
        columns = []
        for k in range(TRACK):
            hit = gs == jnp.broadcast_to(lb[xx, pl.ds(k * 8 + zz, 1), :], (8, 128))
            tiles = []
            for part in range(2):
                for c in range(6):
                    row = vb[pl.ds(((part * TRACK + k) * 6 + c) * 8 + zz, 1), :]
                    tiles.append(jnp.where(hit, jnp.broadcast_to(row, (8, 128)), 0.0))
            columns.append(jnp.concatenate(tiles, axis=0).astype(BF16))
        left = jnp.concatenate(columns, axis=1)
        out = lax.dot_general(left, ohb[xx * 8 + zz], TRANSPOSED, preferred_element_type=F32)
        out = out[:48] + out[48:]
        for c in range(6):
            dense[pl.ds(xx * 384 + c * 8 + zz, 8, stride=48), :] = out[c * 8:c * 8 + 8]

    def hold(k, c, value):
        high = value.astype(BF16).astype(F32)
        vb[pl.ds((k * 6 + c) * 8, 8), :] = high
        vb[pl.ds(((TRACK + k) * 6 + c) * 8, 8), :] = value - high

    def grad_part(i, carry):
        xx = step(x, turn(i), NX)
        for k in range(TRACK):
            e0 = sb[xx, pl.ds((72 + 2 * k) * 8, 8), :]
            e1 = sb[xx, pl.ds((73 + 2 * k) * 8, 8), :]
            for c in range(6):
                hold(k, c, cam_tile(xx, 2 * k, c) * e0 + cam_tile(xx, 2 * k + 1, c) * e1)
        locals_of = lax.broadcasted_iota(jnp.int32, (128, 128), 0).astype(F32)
        for zz in range(NZ):
            for k in range(TRACK):
                label = lb[xx, pl.ds((4 + k) * 8 + zz, 1), :]
                ohb[xx * 8 + zz, :, pl.ds(k * 128, 128)] = (
                    locals_of == jnp.broadcast_to(label, (128, 128))
                ).astype(F32).astype(BF16)
            spread(xx, zz, gbuf)
        sum_core(28, gbuf, in1g, i, xx).start()
        return carry

    def schur(xx):
        for zz in range(NZ):
            for c in range(6):
                tt[zz, pl.ds(c, 8, stride=8), :] = dirs[pl.ds(xx * 384 + c * 8 + zz, 8, stride=48), :]
            high, low = split(tt[zz])
            onehot = ohb[xx * 8 + zz]
            got = jnp.dot(
                jnp.concatenate([high, low], axis=1),
                jnp.concatenate([onehot, onehot], axis=0),
                preferred_element_type=F32,
            )
            for k in range(TRACK):
                group = jnp.broadcast_to(lb[xx, pl.ds(k * 8 + zz, 1), :], (8, 128))
                mine = jnp.zeros((8, 128), F32)
                for g in range(8):
                    mine += jnp.where(
                        group == g, got[g * 8:g * 8 + 8, k * 128:(k + 1) * 128], 0.0
                    )
                db[pl.ds(k * 64 + zz, 8, stride=8), :] = mine
        image = []
        for k in range(TRACK):
            for i in range(2):
                image.append(
                    sum(
                        cam_tile(xx, 2 * k + i, c) * db[pl.ds((k * 8 + c) * 8, 8), :]
                        for c in range(6)
                    )
                )

        def point_tile(kk, j):
            return sb[xx, pl.ds((48 + j * 8 + kk) * 8, 8), :]

        through = [sum(point_tile(kk, j) * image[kk] for kk in range(8)) for j in range(3)]
        image = [image[kk] - sum(point_tile(kk, j) * through[j] for j in range(3)) for kk in range(8)]
        for k in range(TRACK):
            for c in range(6):
                hold(
                    k, c,
                    cam_tile(xx, 2 * k, c) * image[2 * k]
                    + cam_tile(xx, 2 * k + 1, c) * image[2 * k + 1],
                )
        for zz in range(NZ):
            spread(xx, zz, sbuf)

    lax.fori_loop(0, NX, grad_part, 0)

    def pass_on(i):
        r = turn(i)
        xx = step(x, r, NX)
        for d in range(NY):
            sent = 8 + (NX - r) % NX * NY + (NY - d) % NY
            yy = step(y, d, NY)
            part = rows(dirs, ((xx * NC + core) * NY + yy) * 48, 48)
            arrived = copy(p0, part, sent, device(xx, yy, z, core)).wait_recv
            if d == 0:
                pl.when(r > 0)(arrived)
            else:
                arrived()
        gather_core(i, xx).start()

    def send_blocks(base1, base2, dense, in1, r1, in2, i):
        r = turn(i)
        xx = step(x, r, NX)
        sum_core(base1, dense, in1, i, xx).wait()
        here = pl.ds(pl.multiple_of(xx * 192, 8), 192)
        r1[here, :] = dense[pl.ds(pl.multiple_of((xx * NC + core) * 192, 8), 192), :] + in1[here, :]
        for d in (2, 1, 3, 0):
            item = sum_plane(base2, r1, in2, r, d)
            if d == 0:
                pl.when(r > 0)(item.start)
            else:
                item.start()

    def schur_part(i, carry):
        xx = step(x, turn(i), NX)

        @pl.when(i < 2)
        def _():
            pass_on(i + 2)

        gather_core(i, xx).wait()

        schur(xx)

        sum_core(32, sbuf, in1s, i, xx).start()

        @pl.when(i >= 2)
        def _():
            send_blocks(32, 52, sbuf, in1s, r1s, in2s, i - 2)

        return carry

    def send_grad(i, carry):
        send_blocks(28, 36, gbuf, in1g, r1g, in2g, i)
        return carry

    pass_on(0)
    pass_on(1)
    lax.fori_loop(0, NX, send_grad, 0)
    lax.fori_loop(0, NX, schur_part, 0)
    send_blocks(32, 52, sbuf, in1s, r1s, in2s, 2)
    send_blocks(32, 52, sbuf, in1s, r1s, in2s, 3)

    def block(at):
        return pl.ds(pl.multiple_of(at * 48, 8), 48)

    def from_source(r, d):
        return block(step(x, NX - r, NX) * NY + step(y, NY - d, NY))

    def fold_grad():
        total = r1g[block(x * NY + y), :]
        for r, d in plane:
            sum_plane(36, r1g, in2g, r, d).wait()
            total += in2g[from_source(r, d), :]
        return total

    def fold_prod():
        total = r1s[block(x * NY + y), :]
        for r in (0, 1, 3, 2):
            for d in range(NY):
                if r + d > 0:
                    sum_plane(52, r1s, in2s, r, d).wait()
                    total += in2s[from_source(r, d), :]
        return total

    for part, total in enumerate((fold_grad(), fold_prod())):
        r3[...] = total
        for zz in range(NZ):
            r4[pl.ds(zz * 16 + 8 * part, 6), :] = r3[pl.ds(zz, 6, stride=8), :]
    for item in sum_z():
        item.start()
    total = r4[pl.ds(pl.multiple_of(z * 16, 8), 16), :]
    for item in sum_z():
        item.wait()
    for d in range(1, NZ):
        total += in4[pl.ds(pl.multiple_of(step(z, d, NZ) * 16, 8), 16), :]
    for r, d in plane:
        gather_plane(r, d).wait_send()
    os_ref[...] = total


def shards(jac_cam, jac_pt, resid, point_damping, cluster, cam_local, direction, cam_damping):
    def buffer(*shape):
        return pltpu.VMEM(shape, F32)

    scratch = [
        buffer(48, POINTS), buffer(24, POINTS), buffer(8, POINTS), buffer(1, POINTS),
        pltpu.VMEM((1, POINTS), jnp.int32), pltpu.VMEM((TRACK, POINTS), jnp.int32),
        buffer(6, 128), buffer(1, 128),
        pltpu.VMEM((1, POINTS), jnp.int32), pltpu.VMEM((NX * ROWS, POINTS), BF16),
        buffer(NX, 640, 128), buffer(NX, 64, 128), buffer(256, 128), buffer(384, 128),
        pltpu.VMEM((32, 128, 512), BF16), buffer(8, 64, 128),
        buffer(64, 128), buffer(48, 128), buffer(1536, 128),
        buffer(1536, 128), buffer(1536, 128), buffer(768, 128), buffer(768, 128),
        buffer(768, 128), buffer(768, 128), buffer(768, 128), buffer(768, 128),
        buffer(48, 128), buffer(128, 128), buffer(128, 128),
        pltpu.SemaphoreType.DMA((76,)), pltpu.SemaphoreType.DMA((76,)),
        pltpu.SemaphoreType.DMA((45,)),
    ]
    whole = pl.BlockSpec(memory_space=pltpu.VMEM)
    shape = jax.ShapeDtypeStruct((6, 128), F32)
    both = pl.pallas_call(
        kernel,
        out_shape=jax.ShapeDtypeStruct((16, 128), F32),
        in_specs=[pl.BlockSpec(memory_space=pltpu.HBM)] * 8,
        out_specs=whole,
        scratch_shapes=scratch,
        compiler_params=pltpu.CompilerParams(
            collective_id=0, has_side_effects=True, vmem_limit_bytes=62 * 1024 * 1024
        ),
    )(
        jnp.transpose(jac_cam, (0, 2, 1, 3)),
        jnp.transpose(jac_pt, (0, 2, 1, 3)),
        resid,
        point_damping.reshape(1, POINTS),
        cluster.T,
        cam_local.T,
        direction,
        cam_damping.reshape(1, 128),
    )
    return both[:6], cam_damping[None, :] * direction + both[8:14]


def solution(mesh):
    in_specs = (
        P(None, None, None, ("pts", "cam")),
        P(None, None, None, ("pts", "cam")),
        P(None, None, ("pts", "cam")),
        P(("pts", "cam")),
        P(("pts", "cam"), None),
        P(("pts", "cam"), None),
        P(None, ("pts", "cam")),
        P(("pts", "cam")),
    )
    out_specs = (P(None, ("pts", "cam")), P(None, ("pts", "cam")))
    return jax.shard_map(shards, mesh=mesh, in_specs=in_specs, out_specs=out_specs, check_vma=False)
```

```python
import jax
import jax.numpy as jnp
from jax import lax
from jax.experimental import pallas as pl
from jax.experimental.pallas import tpu as pltpu
from jax.sharding import PartitionSpec as P

MESH = pl.DeviceIdType.MESH
F32 = jnp.float32
BF16 = jnp.bfloat16
NX, NY, NZ, NC = 4, 4, 8, 2
POINTS = 2048
CHUNK = 256
ROWS = 176
TRACK = 4
TRANSPOSED = (((1,), (1,)), ((), ()))


def split(value):
    high = value.astype(BF16)
    low = (value - high.astype(F32)).astype(BF16)
    return high, low


def kernel(
    jc_ref, jp_ref, rs_ref, damp_ref, clu_ref, loc_ref, dir_ref, cdamp_ref,
    os_ref,
    at, bt, rt, damp, clu, loc, own, cdamp,
    srow, lhs, sb, lb, db, vb, ohb, tt,
    zb, p0, dirs,
    gbuf, sbuf, in1g, in1s, r1g, r1s, in2g, in2s, r3, r4, in4,
    send, recv, fetch,
):
    me = lax.axis_index("pts")
    y = lax.axis_index("cam")
    core = lax.rem(me, NC)
    z = lax.rem(lax.div(me, NC), NZ)
    x = lax.div(me, NC * NZ)

    def device(xx, yy, zz, cc):
        return {"pts": (xx * NZ + zz) * NC + cc, "cam": yy}

    def step(at, d, size):
        return lax.rem(at + d, size)

    def rows(ref, start, count):
        return ref.at[pl.ds(pl.multiple_of(start, 8), count), :]

    def copy(src, dst, sem, dev):
        return pltpu.make_async_remote_copy(
            src_ref=src, dst_ref=dst, send_sem=send.at[sem], recv_sem=recv.at[sem],
            device_id=dev, device_id_type=MESH,
        )

    barrier = pltpu.get_barrier_semaphore()
    plane = [(r, d) for r in range(NX) for d in range(NY) if r + d > 0]
    peers = [device(x, y, step(z, d, NZ), core) for d in (4, 3, 5)]
    peers += [
        device(step(x, r, NX), step(y, d, NY), z, core)
        for r in (2, 1, 3, 0) for d in (2, 1, 3, 0) if r + d > 0
    ]
    peers += [device(x, y, step(z, d, NZ), core) for d in (2, 6, 1, 7)]
    peers += [device(x, y, z, 1 - core)]
    for dev in peers:
        pl.semaphore_signal(barrier, inc=1, device_id=dev, device_id_type=MESH)

    fetches = [(dir_ref, own), (clu_ref, clu), (loc_ref, loc), (damp_ref, damp), (cdamp_ref, cdamp)]
    fetches += [(rs_ref.at[k], rt.at[pl.ds(2 * k, 2), :]) for k in range(TRACK)]
    fetches += [
        (jp_ref.at[k, j], bt.at[pl.ds(8 * j + 2 * k, 2), :]) for k in range(TRACK) for j in range(3)
    ]
    fetches += [
        (jc_ref.at[k, c], at.at[pl.ds((k * 6 + c) * 2, 2), :]) for k in range(TRACK) for c in range(6)
    ]
    fetches = [
        pltpu.make_async_copy(src, dst, fetch.at[i]) for i, (src, dst) in enumerate(fetches)
    ]
    for item in fetches:
        item.start()
    tt[...] = jnp.zeros_like(tt)
    r4[...] = jnp.zeros_like(r4)

    def gather_z():
        return [
            copy(dir_ref, rows(zb, z * 8, 6), d - 1, device(x, y, step(z, d, NZ), core))
            for d in (4, 3, 5, 2, 6, 1, 7)
        ]

    def gather_plane(r, d):
        there = device(step(x, r, NX), step(y, d, NY), z, core)
        return copy(p0, rows(dirs, ((x * NC + core) * NY + y) * 48, 48), 8 + r * NY + d, there)

    def gather_core(i, xx):
        part = rows(dirs, (xx * NC + core) * 192, 192)
        return copy(part, part, 24 + i, device(x, y, z, 1 - core))

    def sum_core(base, dense, in1, i, xx):
        return copy(
            rows(dense, (xx * NC + 1 - core) * 192, 192), rows(in1, xx * 192, 192),
            base + i, device(x, y, z, 1 - core),
        )

    def sum_plane(base, r1, in2, r, d):
        xx, yy = step(x, r, NX), step(y, d, NY)
        return copy(
            rows(r1, (xx * NY + yy) * 48, 48), rows(in2, (x * NY + y) * 48, 48),
            base + r * NY + d, device(xx, yy, z, core),
        )

    def sum_z():
        return [
            copy(rows(r4, step(z, d, NZ) * 16, 16), rows(in4, z * 16, 16), 68 + d,
                 device(x, y, step(z, d, NZ), core))
            for d in (4, 3, 5, 2, 6, 1, 7)
        ]

    def turn(i):
        return (i + 2) % NX

    pl.semaphore_wait(barrier, len(peers))
    for item in gather_z():
        item.start()
    for item in fetches:
        item.wait()

    lane = lax.broadcasted_iota(jnp.int32, (CHUNK, CHUNK + 128), 1)
    before = (
        (lax.broadcasted_iota(jnp.int32, (CHUNK, CHUNK + 128), 0) < lane) | (lane >= CHUNK)
    ).astype(F32).astype(BF16)

    def eliminate(b, seen):
        here = pl.ds(pl.multiple_of(b * CHUNK, CHUNK), CHUNK)
        cluster = clu[:, here]
        member = (
            lax.broadcasted_iota(jnp.int32, (64, CHUNK), 0) == jnp.broadcast_to(cluster, (64, CHUNK))
        ).astype(F32)
        counts = jnp.dot(member.astype(BF16), before, preferred_element_type=F32)
        ahead = counts[:, :CHUNK] + jnp.concatenate([seen, seen], axis=1)
        position = jnp.sum(member * ahead, axis=0, keepdims=True)
        slot = jnp.bitwise_and(cluster, 15) * 64 + position.astype(jnp.int32)
        srow[:, here] = slot
        quarter = lax.shift_right_logical(cluster, 4)

        b0, b1, b2 = (bt[pl.ds(8 * j, 8), here] for j in range(3))
        res = rt[:, here]

        def total(value):
            return jnp.sum(value, axis=0, keepdims=True)

        extra = damp[:, here]
        n00, n10, n20 = total(b0 * b0) + extra, total(b1 * b0), total(b2 * b0)
        n11, n21, n22 = total(b1 * b1) + extra, total(b2 * b1), total(b2 * b2) + extra
        q0, q1, q2 = total(b0 * res), total(b1 * res), total(b2 * res)
        ia = 1.0 / jnp.sqrt(n00)
        ba, ca = n10 * ia, n20 * ia
        ib = 1.0 / jnp.sqrt(n11 - ba * ba)
        cb = (n21 - ca * ba) * ib
        ic = 1.0 / jnp.sqrt(n22 - ca * ca - cb * cb)
        c0 = b0 * ia
        c1 = (b1 - ba * c0) * ib
        c2 = (b2 - ca * c0 - cb * c1) * ic
        s0 = q0 * ia
        s1 = (q1 - ba * s0) * ib
        s2 = (q2 - ca * s0 - cb * s1) * ic
        rest = res - (c0 * s0 + c1 * s1 + c2 * s2)

        masks = [
            jnp.broadcast_to((quarter == f).astype(F32), (16, CHUNK)).astype(BF16)
            for f in range(NX)
        ]

        def put(base, value):
            for f in range(NX):
                lhs[pl.ds(f * ROWS + base, 16), here] = value * masks[f]

        for base in range(0, 48, 16):
            high, low = split(at[pl.ds(base, 16), here])
            put(base, high)
            put(80 + base, low)
        for base, pair in ((48, (c0, c1)), (64, (c2, rest))):
            high, low = split(jnp.concatenate(pair, axis=0))
            put(base, high)
            put(80 + base, low)
        label = loc[:, here]
        parts = [
            lax.shift_right_logical(label, 7).astype(F32),
            jnp.bitwise_and(label, 127).astype(F32),
            jnp.zeros((8, CHUNK), F32),
        ]
        put(160, jnp.concatenate(parts, axis=0).astype(BF16))
        return seen + counts[:, CHUNK:]

    lax.fori_loop(0, POINTS // CHUNK, eliminate, jnp.zeros((64, 128), F32))

    half = jnp.where(lax.broadcasted_iota(jnp.int32, (8, 128), 1) >= 64, 4.0, 0.0)
    half = jnp.where(lax.broadcasted_iota(jnp.int32, (8, 128), 0) < 4, half, 0.0)

    def sort(q, carry):
        slots = lax.broadcasted_iota(jnp.int32, (256, POINTS), 0) + q * 256
        place = (slots == jnp.broadcast_to(srow[...], (256, POINTS))).astype(F32).astype(BF16)
        out = lax.dot_general(lhs[...], place, TRANSPOSED, preferred_element_type=F32)
        for xx in range(NX):
            for zz in range(2):
                part = out[xx * ROWS:(xx + 1) * ROWS, zz * 128:(zz + 1) * 128]
                sb[xx, pl.ds(2 * q + zz, 80, stride=8), :] = part[:80] + part[80:160]
                lb[xx, pl.ds(2 * q + zz, 8, stride=8), :] = part[160:168] + half
        return carry

    lax.fori_loop(0, 2, sort, 0)
    for item in gather_z():
        item.wait()
    zb[pl.ds(pl.multiple_of(z * 8, 8), 6), :] = own[...]
    for zz in range(NZ):
        p0[pl.ds(zz, 6, stride=8), :] = zb[pl.ds(zz * 8, 6), :]
    for r in (2, 1, 3, 0):
        for d in (2, 1, 3, 0):
            if r + d > 0:
                gather_plane(r, d).start()
    dirs[pl.ds(pl.multiple_of(((x * NC + core) * NY + y) * 48, 8), 48), :] = p0[...]
    lax.fori_loop(2, 4, sort, 0)

    def cam_tile(xx, kk, c):
        return sb[xx, pl.ds(((kk // 2 * 6 + c) * 2 + kk % 2) * 8, 8), :]

    def spread(xx, zz, dense):
        gs = lax.broadcasted_iota(jnp.int32, (8, 128), 0).astype(F32)
        columns = []
        for k in range(TRACK):
            hit = gs == jnp.broadcast_to(lb[xx, pl.ds(k * 8 + zz, 1), :], (8, 128))
            tiles = []
            for part in range(2):
                for c in range(6):
                    row = vb[pl.ds(((part * TRACK + k) * 6 + c) * 8 + zz, 1), :]
                    tiles.append(jnp.where(hit, jnp.broadcast_to(row, (8, 128)), 0.0))
            columns.append(jnp.concatenate(tiles, axis=0).astype(BF16))
        left = jnp.concatenate(columns, axis=1)
        out = lax.dot_general(left, ohb[xx * 8 + zz], TRANSPOSED, preferred_element_type=F32)
        out = out[:48] + out[48:]
        for c in range(6):
            dense[pl.ds(xx * 384 + c * 8 + zz, 8, stride=48), :] = out[c * 8:c * 8 + 8]

    def hold(k, c, value):
        high = value.astype(BF16).astype(F32)
        vb[pl.ds((k * 6 + c) * 8, 8), :] = high
        vb[pl.ds(((TRACK + k) * 6 + c) * 8, 8), :] = value - high

    def grad_part(i, carry):
        xx = step(x, turn(i), NX)
        for k in range(TRACK):
            e0 = sb[xx, pl.ds((72 + 2 * k) * 8, 8), :]
            e1 = sb[xx, pl.ds((73 + 2 * k) * 8, 8), :]
            for c in range(6):
                hold(k, c, cam_tile(xx, 2 * k, c) * e0 + cam_tile(xx, 2 * k + 1, c) * e1)
        locals_of = lax.broadcasted_iota(jnp.int32, (128, 128), 0).astype(F32)
        for zz in range(NZ):
            for k in range(TRACK):
                label = lb[xx, pl.ds((4 + k) * 8 + zz, 1), :]
                ohb[xx * 8 + zz, :, pl.ds(k * 128, 128)] = (
                    locals_of == jnp.broadcast_to(label, (128, 128))
                ).astype(F32).astype(BF16)
            spread(xx, zz, gbuf)
        sum_core(28, gbuf, in1g, i, xx).start()
        return carry

    def schur(xx):
        for zz in range(NZ):
            for c in range(6):
                tt[zz, pl.ds(c, 8, stride=8), :] = dirs[pl.ds(xx * 384 + c * 8 + zz, 8, stride=48), :]
            high, low = split(tt[zz])
            onehot = ohb[xx * 8 + zz]
            got = jnp.dot(
                jnp.concatenate([high, low], axis=1),
                jnp.concatenate([onehot, onehot], axis=0),
                preferred_element_type=F32,
            )
            for k in range(TRACK):
                group = jnp.broadcast_to(lb[xx, pl.ds(k * 8 + zz, 1), :], (8, 128))
                mine = jnp.zeros((8, 128), F32)
                for g in range(8):
                    mine += jnp.where(
                        group == g, got[g * 8:g * 8 + 8, k * 128:(k + 1) * 128], 0.0
                    )
                db[pl.ds(k * 64 + zz, 8, stride=8), :] = mine
        image = []
        for k in range(TRACK):
            for i in range(2):
                image.append(
                    sum(
                        cam_tile(xx, 2 * k + i, c) * db[pl.ds((k * 8 + c) * 8, 8), :]
                        for c in range(6)
                    )
                )

        def point_tile(kk, j):
            return sb[xx, pl.ds((48 + j * 8 + kk) * 8, 8), :]

        through = [sum(point_tile(kk, j) * image[kk] for kk in range(8)) for j in range(3)]
        image = [image[kk] - sum(point_tile(kk, j) * through[j] for j in range(3)) for kk in range(8)]
        for k in range(TRACK):
            for c in range(6):
                hold(
                    k, c,
                    cam_tile(xx, 2 * k, c) * image[2 * k]
                    + cam_tile(xx, 2 * k + 1, c) * image[2 * k + 1],
                )
        for zz in range(NZ):
            spread(xx, zz, sbuf)

    lax.fori_loop(0, NX, grad_part, 0)

    def pass_on(i):
        r = turn(i)
        xx = step(x, r, NX)
        for d in range(NY):
            sent = 8 + (NX - r) % NX * NY + (NY - d) % NY
            yy = step(y, d, NY)
            part = rows(dirs, ((xx * NC + core) * NY + yy) * 48, 48)
            arrived = copy(p0, part, sent, device(xx, yy, z, core)).wait_recv
            if d == 0:
                pl.when(r > 0)(arrived)
            else:
                arrived()
        gather_core(i, xx).start()

    def send_blocks(base1, base2, dense, in1, r1, in2, i):
        r = turn(i)
        xx = step(x, r, NX)
        sum_core(base1, dense, in1, i, xx).wait()
        here = pl.ds(pl.multiple_of(xx * 192, 8), 192)
        r1[here, :] = dense[pl.ds(pl.multiple_of((xx * NC + core) * 192, 8), 192), :] + in1[here, :]
        for d in (2, 1, 3, 0):
            item = sum_plane(base2, r1, in2, r, d)
            if d == 0:
                pl.when(r > 0)(item.start)
            else:
                item.start()

    def schur_part(i, carry):
        xx = step(x, turn(i), NX)

        @pl.when(i < 2)
        def _():
            pass_on(i + 2)

        gather_core(i, xx).wait()

        schur(xx)

        sum_core(32, sbuf, in1s, i, xx).start()

        @pl.when(i >= 2)
        def _():
            send_blocks(32, 52, sbuf, in1s, r1s, in2s, i - 2)

        return carry

    def send_grad(i, carry):
        send_blocks(28, 36, gbuf, in1g, r1g, in2g, i)
        return carry

    pass_on(0)
    pass_on(1)
    lax.fori_loop(0, NX, send_grad, 0)
    lax.fori_loop(0, NX, schur_part, 0)
    send_blocks(32, 52, sbuf, in1s, r1s, in2s, 2)
    send_blocks(32, 52, sbuf, in1s, r1s, in2s, 3)

    def block(at):
        return pl.ds(pl.multiple_of(at * 48, 8), 48)

    def from_source(r, d):
        return block(step(x, NX - r, NX) * NY + step(y, NY - d, NY))

    def fold_grad():
        total = r1g[block(x * NY + y), :]
        for r, d in plane:
            sum_plane(36, r1g, in2g, r, d).wait()
            total += in2g[from_source(r, d), :]
        return total

    def fold_prod():
        total = r1s[block(x * NY + y), :]
        for r in (0, 1, 3, 2):
            for d in range(NY):
                if r + d > 0:
                    sum_plane(52, r1s, in2s, r, d).wait()
                    total += in2s[from_source(r, d), :]
        return total

    for part, total in enumerate((fold_grad(), fold_prod())):
        r3[...] = total
        for zz in range(NZ):
            r4[pl.ds(zz * 16 + 8 * part, 6), :] = r3[pl.ds(zz, 6, stride=8), :]
    for item in sum_z():
        item.start()
    total = r4[pl.ds(pl.multiple_of(z * 16, 8), 16), :]
    for item in sum_z():
        item.wait()
    for d in range(1, NZ):
        total += in4[pl.ds(pl.multiple_of(step(z, d, NZ) * 16, 8), 16), :]
    for r, d in plane:
        gather_plane(r, d).wait_send()
    os_ref[...] = total


def shards(jac_cam, jac_pt, resid, point_damping, cluster, cam_local, direction, cam_damping):
    def buffer(*shape):
        return pltpu.VMEM(shape, F32)

    scratch = [
        buffer(48, POINTS), buffer(24, POINTS), buffer(8, POINTS), buffer(1, POINTS),
        pltpu.VMEM((1, POINTS), jnp.int32), pltpu.VMEM((TRACK, POINTS), jnp.int32),
        buffer(6, 128), buffer(1, 128),
        pltpu.VMEM((1, POINTS), jnp.int32), pltpu.VMEM((NX * ROWS, POINTS), BF16),
        buffer(NX, 640, 128), buffer(NX, 64, 128), buffer(256, 128), buffer(384, 128),
        pltpu.VMEM((32, 128, 512), BF16), buffer(8, 64, 128),
        buffer(64, 128), buffer(48, 128), buffer(1536, 128),
        buffer(1536, 128), buffer(1536, 128), buffer(768, 128), buffer(768, 128),
        buffer(768, 128), buffer(768, 128), buffer(768, 128), buffer(768, 128),
        buffer(48, 128), buffer(128, 128), buffer(128, 128),
        pltpu.SemaphoreType.DMA((76,)), pltpu.SemaphoreType.DMA((76,)),
        pltpu.SemaphoreType.DMA((45,)),
    ]
    whole = pl.BlockSpec(memory_space=pltpu.VMEM)
    shape = jax.ShapeDtypeStruct((6, 128), F32)
    both = pl.pallas_call(
        kernel,
        out_shape=jax.ShapeDtypeStruct((16, 128), F32),
        in_specs=[pl.BlockSpec(memory_space=pltpu.HBM)] * 8,
        out_specs=whole,
        scratch_shapes=scratch,
        compiler_params=pltpu.CompilerParams(
            collective_id=0, has_side_effects=True, vmem_limit_bytes=62 * 1024 * 1024
        ),
    )(
        jnp.transpose(jac_cam, (0, 2, 1, 3)),
        jnp.transpose(jac_pt, (0, 2, 1, 3)),
        resid,
        point_damping.reshape(1, POINTS),
        cluster.T,
        cam_local.T,
        direction,
        cam_damping.reshape(1, 128),
    )
    return both[:6], cam_damping[None, :] * direction + both[8:14]


def solution(mesh):
    in_specs = (
        P(None, None, None, ("pts", "cam")),
        P(None, None, None, ("pts", "cam")),
        P(None, None, ("pts", "cam")),
        P(("pts", "cam")),
        P(("pts", "cam"), None),
        P(("pts", "cam"), None),
        P(None, ("pts", "cam")),
        P(("pts", "cam")),
    )
    out_specs = (P(None, ("pts", "cam")), P(None, ("pts", "cam")))
    return jax.shard_map(shards, mesh=mesh, in_specs=in_specs, out_specs=out_specs, check_vma=False)
```
